32 devices in a mesh: dp: 8 (over z, y), mp: 4 (over x, core).
Axes of the slice: x: 2, y: 2, z: 4, core: 2. Of those that a mesh axis runs over, the one named last changes fastest.
Arguments:
- captions: bfloat16 [512, 16, 768], P('dp'), may hold values from -6 to 6
- token_ids: int32 [512, 16], P('dp'), may hold values from 0 to 49407, as said below
- pairing: int32 [512], P('dp'), may hold values from 0 to 511, each once
- low_images: bfloat16 [64, 50, 768], P(('dp', 'mp')), may hold values from -6 to 6
- high_images: bfloat16 [448, 145, 768], P(('dp', 'mp')), may hold values from -6 to 6
- frozen_qkv: bfloat16 [3, 768, 768], replicated, may hold values from -0.21875 to 0.21875
- frozen_out: bfloat16 [768, 768], replicated, may hold values from -1.75 to 1.75
- frozen_up: bfloat16 [768, 3072], replicated, may hold values from -0.21875 to 0.21875
- frozen_down: bfloat16 [3072, 768], replicated, may hold values from -0.109375 to 0.109375
- frozen_gains: float32 [2, 768], replicated, may hold values from 0.5 to 1.5
- master_qkv: float32 [3, 768, 768], P(None, 'dp', 'mp'), may hold values from -0.21875 to 0.21875
- master_out: float32 [768, 768], P('mp', 'dp'), may hold values from -0.625 to 0.625
- master_up: float32 [768, 3072], P('dp', 'mp'), may hold values from -0.21875 to 0.21875
- master_down: float32 [3072, 768], P('mp', 'dp'), may hold values from -0.109375 to 0.109375
- master_norms: float32 [4, 768], P(None, 'dp'), may hold values from -0.9 to 1.3, as said below
- first_qkv: float32 [3, 768, 768], P(None, 'dp', 'mp')
- first_out: float32 [768, 768], P('mp', 'dp')
- first_up: float32 [768, 3072], P('dp', 'mp')
- first_down: float32 [3072, 768], P('mp', 'dp')
- first_norms: float32 [4, 768], P(None, 'dp')
- second_qkv: float32 [3, 768, 768], P(None, 'dp', 'mp'), as said below
- second_out: float32 [768, 768], P('mp', 'dp'), as said below
- second_up: float32 [768, 3072], P('dp', 'mp'), as said below
- second_down: float32 [3072, 768], P('mp', 'dp'), as said below
- second_norms: float32 [4, 768], P(None, 'dp'), as said below
Outputs:
- input_grad: float32 [512, 16, 768], P('dp')
- grad_qkv: float32 [3, 768, 768], P(None, 'dp', 'mp')
- grad_out: float32 [768, 768], P('mp', 'dp')
- grad_up: float32 [768, 3072], P('dp', 'mp')
- grad_down: float32 [3072, 768], P('mp', 'dp')
- grad_norms: float32 [4, 768], P(None, 'dp')
- new_qkv: float32 [3, 768, 768], P(None, 'dp', 'mp')
- new_out: float32 [768, 768], P('mp', 'dp')
- new_up: float32 [768, 3072], P('dp', 'mp')
- new_down: float32 [3072, 768], P('mp', 'dp')
- new_norms: float32 [4, 768], P(None, 'dp')
- copy_qkv: bfloat16 [3, 768, 768], P(None, 'dp', 'mp')
- copy_out: bfloat16 [768, 768], P('mp', 'dp')
- copy_up: bfloat16 [768, 3072], P('dp', 'mp')
- copy_down: bfloat16 [3072, 768], P('mp', 'dp')
- copy_norms: bfloat16 [4, 768], P(None, 'dp')
- mean_qkv: float32 [3, 768, 768], P(None, 'dp', 'mp')
- mean_out: float32 [768, 768], P('mp', 'dp')
- mean_up: float32 [768, 3072], P('dp', 'mp')
- mean_down: float32 [3072, 768], P('mp', 'dp')
- mean_norms: float32 [4, 768], P(None, 'dp')
- square_qkv: float32 [3, 768, 768], P(None, 'dp', 'mp')
- square_out: float32 [768, 768], P('mp', 'dp')
- square_up: float32 [768, 3072], P('dp', 'mp')
- square_down: float32 [3072, 768], P('mp', 'dp')
- square_norms: float32 [4, 768], P(None, 'dp')
- matrix_norms: float32 [2, 10], replicated
The draws below stay inside these ranges and needn't reach their ends.
Inputs may be any that keep to these rules, and one draw needn't show every extreme that they name: `token_ids`: each caption is a run of nonzero ids followed by zeros, with 4 to 16 nonzero ids; some caption has all 16 tokens nonzero. A permutation: caption c is paired with image pairing[c]. `master_norms`: rows 0 and 2 are gains, rows 1 and 3 shifts. `second_qkv`: every entry is positive. `second_out`: every entry is positive. `second_up`: every entry is positive. `second_down`: every entry is positive. `second_norms`: every entry is positive.
All inputs are finite; a program needn't handle non-finite values.
Results may differ from the reference program's by a relative error of at most 0.012.
The reference program's roundings to bfloat16 on the way count: a program that leaves them out, or rounds other values in their place, can miss the bound.
Values may be sent and summed in bfloat16 or wider, within the bound.
A program may use at most 192 MiB of HBM per device.

```python
import math
import jax
import jax.numpy as jnp
from jax import lax

D = 768
FF = 3072
HEADS = 12
HEAD_DIM = 64
VOCAB = 49408
SEQ = 16
LOW_ROWS = 50
HIGH_ROWS = 145
STEP = 5
LO_DEV = 2
HI_DEV = 14
CAPTIONS = 512
LOW_IMGS = 64
HIGH_IMGS = 448
DEVICES = 32


def grad_size():
    return 150.0 / (D * math.sqrt(CAPTIONS * SEQ))


def first_moment(key, shape, size):
    values = jnp.clip(jax.random.normal(key, shape, jnp.float32), -4.0, 4.0)
    return values * (size / 9.0)


def second_moment(key, shape, size):
    factor = jnp.exp(jax.random.uniform(key, shape, jnp.float32, 0.0, math.log(4.0)))
    return factor * (size * size / 999.0)


def draw_token_ids(key, part):
    lengths = jax.random.randint(jax.random.fold_in(key, 11), (CAPTIONS,), 4, SEQ + 1)
    lengths = lengths.at[0].set(SEQ)
    tokens = jax.random.randint(jax.random.fold_in(key, 12), (CAPTIONS, SEQ), 1, VOCAB)
    tokens = tokens.at[0, 0].set(VOCAB - 1)
    position = jnp.arange(SEQ, dtype=jnp.int32)[None, :]
    return jnp.where(position < lengths[:, None], tokens, 0).astype(jnp.int32)


def draw_master_norms(key, part):
    gains = jax.random.uniform(jax.random.fold_in(key, 21), (4, D), jnp.float32, 0.8, 1.2)
    shifts = 0.3 * jnp.clip(jax.random.normal(jax.random.fold_in(key, 22), (4, D), jnp.float32), -3.0, 3.0)
    parity = jnp.arange(4, dtype=jnp.int32)[:, None] % 2
    return jnp.where(parity == 0, gains, shifts)


def draw_first_qkv(key, part):
    return first_moment(key, (3, D, D), grad_size())


def draw_first_out(key, part):
    return first_moment(key, (D, D), grad_size())


def draw_first_up(key, part):
    return first_moment(key, (D, FF), grad_size())


def draw_first_down(key, part):
    return first_moment(key, (FF, D), grad_size())


def draw_first_norms(key, part):
    return first_moment(key, (4, D), 4.0 * grad_size())


def draw_second_qkv(key, part):
    return second_moment(key, (3, D, D), grad_size())


def draw_second_out(key, part):
    return second_moment(key, (D, D), grad_size())


def draw_second_up(key, part):
    return second_moment(key, (D, FF), grad_size())


def draw_second_down(key, part):
    return second_moment(key, (FF, D), grad_size())


def draw_second_norms(key, part):
    return second_moment(key, (4, D), 4.0 * grad_size())


def block_levels(rng, extent, pieces, least, largest):
    def one(dim, parts):
        heights = jax.random.uniform(jax.random.fold_in(jax.random.fold_in(rng, 6), dim), (parts,), jnp.float32, least / len(pieces), largest / len(pieces))
        return jnp.repeat(jnp.exp(heights), extent[dim] // parts).reshape((-1,) + (1,) * (len(extent) - dim - 1))

    factor_of = one(*pieces[0])
    for cut in pieces[1:]:
        factor_of = factor_of * one(*cut)
    return factor_of


def normal_values(own_key, dims, deviation, bound, shards=(), kind=jnp.bfloat16):
    drawn = deviation * jax.random.normal(own_key, dims, jnp.float32)
    if shards:
        drawn = drawn * block_levels(own_key, dims, shards, -0.22, 0.18)
    return jnp.clip(drawn, -bound, bound).astype(kind)


def setup_inputs(seed: int = 0) -> dict:
    arg_keys = jax.random.split(jax.random.key(seed), 26)
    return {
        "captions": normal_values(arg_keys[0], (CAPTIONS, SEQ, D), 1.0, 6.0, ((0, 8),)),
        "token_ids": draw_token_ids(jax.random.fold_in(arg_keys[25], 71), 0),
        "pairing": jax.random.permutation(arg_keys[2], CAPTIONS).astype(jnp.int32),
        "low_images": normal_values(arg_keys[3], (LOW_IMGS, LOW_ROWS, D), 1.0, 6.0, ((0, 32),)),
        "high_images": normal_values(arg_keys[4], (HIGH_IMGS, HIGH_ROWS, D), 1.0, 6.0, ((0, 32),)),
        "frozen_qkv": normal_values(arg_keys[5], (3, D, D), D ** -0.5, 0.21875),
        "frozen_out": normal_values(arg_keys[6], (D, D), (max(D // 64, 8)) ** -0.5, 1.75),
        "frozen_up": normal_values(arg_keys[7], (D, FF), D ** -0.5, 0.21875),
        "frozen_down": normal_values(arg_keys[8], (FF, D), FF ** -0.5, 0.109375),
        "frozen_gains": jnp.clip(1.0 + 0.1 * jax.random.normal(arg_keys[9], (2, D), jnp.float32), 0.5, 1.5),
        "master_qkv": normal_values(arg_keys[10], (3, D, D), D ** -0.5, 0.21875, ((1, 8), (2, 4)), jnp.float32),
        "master_out": normal_values(arg_keys[11], (D, D), (D // 8) ** -0.5, 0.625, ((0, 4), (1, 8)), jnp.float32),
        "master_up": normal_values(arg_keys[12], (D, FF), D ** -0.5, 0.21875, ((0, 8), (1, 4)), jnp.float32),
        "master_down": normal_values(arg_keys[13], (FF, D), FF ** -0.5, 0.109375, ((0, 4), (1, 8)), jnp.float32),
        "master_norms": draw_master_norms(jax.random.fold_in(arg_keys[25], 71), 0),
        "first_qkv": draw_first_qkv(jax.random.fold_in(arg_keys[25], 71), 0),
        "first_out": draw_first_out(jax.random.fold_in(arg_keys[25], 71), 0),
        "first_up": draw_first_up(jax.random.fold_in(arg_keys[25], 71), 0),
        "first_down": draw_first_down(jax.random.fold_in(arg_keys[25], 71), 0),
        "first_norms": draw_first_norms(jax.random.fold_in(arg_keys[25], 71), 0),
        "second_qkv": draw_second_qkv(jax.random.fold_in(arg_keys[25], 71), 0),
        "second_out": draw_second_out(jax.random.fold_in(arg_keys[25], 71), 0),
        "second_up": draw_second_up(jax.random.fold_in(arg_keys[25], 71), 0),
        "second_down": draw_second_down(jax.random.fold_in(arg_keys[25], 71), 0),
        "second_norms": draw_second_norms(jax.random.fold_in(arg_keys[25], 71), 0),
    }


@jax.custom_vjp
def low(v):
    return lax.optimization_barrier(v.astype(jnp.bfloat16)).astype(jnp.float32)

@jax.custom_vjp
def low_back(v):
    return v

def low_keep(v):
    return (low(v), None)

def low_pass(kept, grad):
    return (grad,)

def back_keep(v):
    return (v, None)

def back_low(kept, grad):
    return (low(grad),)
low.defvjp(low_keep, low_pass)
low_back.defvjp(back_keep, back_low)
logit_scale = 48.0
learning_rate = 0.5
weight_decay = 0.01

def matmul_high(left, right):
    return jnp.einsum('...i,ij->...j', left, right, precision=lax.Precision.HIGHEST)

def layer_norm(inputs, gain, shift):
    centre = inputs - lax.optimization_barrier(jnp.mean(inputs, axis=-1, keepdims=True))
    spread = lax.optimization_barrier(jnp.mean(centre * centre, axis=-1, keepdims=True))
    return centre * lax.rsqrt(spread + 1e-05) * gain + shift

def attention(normed, w_query, w_key, w_value, w_output, keep_mask):
    batch_rows, seq_rows, width_all = normed.shape

    def split_heads(weight):
        projected = low(low_back(matmul_high(normed, weight)))
        return projected.reshape(batch_rows, seq_rows, HEADS, HEAD_DIM)
    query_heads = split_heads(w_query)
    key_heads = split_heads(w_key)
    value_heads = split_heads(w_value)
    scores = jnp.einsum('bqhd,bkhd->bhqk', query_heads, key_heads, precision=lax.Precision.HIGHEST) * HEAD_DIM ** (-0.5)
    scores = low_back(jnp.where(keep_mask, scores, -1e+30))
    weights_soft = jax.nn.softmax(scores, axis=-1)
    context = jnp.einsum('bhqk,bkhd->bqhd', low(weights_soft), value_heads, precision=lax.Precision.HIGHEST)
    context = low(low_back(context.reshape(batch_rows, seq_rows, width_all)))
    return low_back(matmul_high(context, w_output))

def feed_forward(normed, w_up, w_down):
    pre_act = low_back(matmul_high(normed, w_up))
    hidden = low(jax.nn.gelu(pre_act, approximate=True))
    return low_back(matmul_high(hidden, w_down))

def block(inputs, params, keep_mask):
    w_query, w_key, w_value, w_output, w_up, w_down, gain_one, shift_one, gain_two, shift_two = params
    after_attn = inputs + attention(low(layer_norm(inputs, gain_one, shift_one)), w_query, w_key, w_value, w_output, keep_mask)
    return after_attn + feed_forward(low(layer_norm(after_attn, gain_two, shift_two)), w_up, w_down)

def text_loss(inputs, masters, alive, pairing, images):
    w_qkv, w_out, w_up, w_down, norm_rows = [low(weight) for weight in masters]
    params = (w_qkv[0], w_qkv[1], w_qkv[2], w_out, w_up, w_down, norm_rows[0], norm_rows[1], norm_rows[2], norm_rows[3])
    causal = jnp.tril(jnp.ones((SEQ, SEQ), dtype=jnp.bool_))

    def embed_block(pair):
        rows, alive_rows = pair
        keep_mask = causal[None, None] & (alive_rows[:, None, None, :] > 0.5)
        outputs = block(rows, params, keep_mask)
        counted = lax.optimization_barrier(jnp.sum(alive_rows, axis=1, keepdims=True))
        pooled = lax.optimization_barrier(jnp.sum(outputs * alive_rows[:, :, None], axis=1)) / counted
        return pooled * lax.rsqrt(lax.optimization_barrier(jnp.sum(pooled * pooled, axis=1, keepdims=True)) + 1e-06)
    block_size = 256 if CAPTIONS % 256 == 0 else CAPTIONS
    block_count = CAPTIONS // block_size
    pooled_all = lax.map(jax.checkpoint(embed_block), (inputs.reshape(block_count, block_size, SEQ, D), alive.reshape(block_count, block_size, SEQ)))
    text = low(pooled_all.reshape(CAPTIONS, D))
    logits = logit_scale * low_back(jnp.dot(text, images.T, precision=lax.Precision.HIGHEST))
    row_lse = jax.nn.logsumexp(logits, axis=1)
    matched = jnp.arange(CAPTIONS, dtype=jnp.int32)[None, :] == pairing[:, None]
    positive = jnp.sum(jnp.where(matched, logits, 0.0))
    return (jnp.sum(row_lse) - positive) / CAPTIONS

def lamb(weight, grad, first, second, axes):
    mean_new = 0.9 * first + 0.1 * grad
    square_new = 0.999 * second + 0.001 * grad * grad
    update = mean_new / (1.0 - 0.9 ** STEP) / (jnp.sqrt(square_new / (1.0 - 0.999 ** STEP)) + 1e-06) + weight_decay * weight
    weight_sq = lax.optimization_barrier(jnp.sum(weight * weight, axis=axes, keepdims=True))
    update_sq = lax.optimization_barrier(jnp.sum(update * update, axis=axes, keepdims=True))
    ratio = jnp.sqrt(weight_sq) / jnp.sqrt(update_sq)
    fresh = weight - learning_rate * ratio * update
    return (fresh, mean_new, square_new, jnp.sqrt(weight_sq).reshape(-1), jnp.sqrt(update_sq).reshape(-1))

def reference(captions, token_ids, pairing, low_images, high_images, frozen_qkv, frozen_out, frozen_up, frozen_down, frozen_gains, master_qkv, master_out, master_up, master_down, master_norms, first_qkv, first_out, first_up, first_down, first_norms, second_qkv, second_out, second_up, second_down, second_norms):
    zero_shift = jnp.zeros((D,), jnp.float32)
    frozen_qkv_f = frozen_qkv.astype(jnp.float32)
    frozen = (frozen_qkv_f[0], frozen_qkv_f[1], frozen_qkv_f[2], frozen_out.astype(jnp.float32), frozen_up.astype(jnp.float32), frozen_down.astype(jnp.float32), frozen_gains[0], zero_shift, frozen_gains[1], zero_shift)

    def image_embed(rows):
        outputs = block(rows.astype(jnp.float32), frozen, True)
        leading = outputs[:, 0, :]
        return low(leading * lax.rsqrt(lax.optimization_barrier(jnp.sum(leading * leading, axis=1, keepdims=True)) + 1e-06))
    low_embed = lax.map(image_embed, low_images.reshape(DEVICES, LO_DEV, LOW_ROWS, D))
    high_embed = lax.map(image_embed, high_images.reshape(DEVICES, HI_DEV, HIGH_ROWS, D))
    images = jnp.concatenate([low_embed, high_embed], axis=1).reshape(CAPTIONS, D)
    alive = (token_ids != 0).astype(jnp.float32)
    masters = (master_qkv, master_out, master_up, master_down, master_norms)
    loss, pull = jax.vjp(lambda inputs, mats: text_loss(inputs, mats, alive, pairing, images), captions.astype(jnp.float32), masters)
    input_grad, grads = pull(jnp.ones_like(loss))
    firsts = (first_qkv, first_out, first_up, first_down, first_norms)
    seconds = (second_qkv, second_out, second_up, second_down, second_norms)
    axes_all = ((1, 2), (0, 1), (0, 1), (0, 1), (1,))
    results = [lamb(masters[index], grads[index], firsts[index], seconds[index], axes_all[index]) for index in range(5)]
    weight_norms = jnp.concatenate([item[3] for item in results])
    update_norms = jnp.concatenate([item[4] for item in results])
    matrix_norms = jnp.stack([weight_norms, update_norms])
    news = [item[0] for item in results]
    copies = [item[0].astype(jnp.bfloat16) for item in results]
    means = [item[1] for item in results]
    squares = [item[2] for item in results]
    return (input_grad, grads[0], grads[1], grads[2], grads[3], grads[4], news[0], news[1], news[2], news[3], news[4], copies[0], copies[1], copies[2], copies[3], copies[4], means[0], means[1], means[2], means[3], means[4], squares[0], squares[1], squares[2], squares[3], squares[4], matrix_norms)
```

```python
from functools import partial
from types import SimpleNamespace

import jax
import jax.numpy as jnp
from jax import lax
from jax.experimental import pallas as pl
from jax.experimental.pallas import tpu as pltpu
from jax.sharding import PartitionSpec as P

HEAD_DIM = 64
STEP = 5


logit_scale = 48.0
learning_rate = 0.5
weight_decay = 0.01


def layer_norm(inputs, gain, shift):
    centre = inputs - jnp.mean(inputs, axis=-1, keepdims=True)
    spread = jnp.mean(centre * centre, axis=-1, keepdims=True)
    return centre * lax.rsqrt(spread + 1e-05) * gain + shift


def frozen_embed(rows, frozen_qkv, frozen_out, frozen_up, frozen_down, frozen_gains):
    batch_rows, seq_rows, width_all = rows.shape
    head_count = width_all // HEAD_DIM
    inputs = rows.astype(jnp.float32)
    normed = layer_norm(inputs, frozen_gains[0], 0.0).astype(jnp.bfloat16)
    projected = jnp.einsum(
        "bld,tde->tble", normed, frozen_qkv, preferred_element_type=jnp.float32
    ).astype(jnp.bfloat16)
    heads_all = projected.reshape(3, batch_rows, seq_rows, head_count, HEAD_DIM)
    scores = jnp.einsum(
        "bqhd,bkhd->bhqk", heads_all[0], heads_all[1], preferred_element_type=jnp.float32
    ) * HEAD_DIM ** (-0.5)
    weights_soft = jax.nn.softmax(scores, axis=-1).astype(jnp.bfloat16)
    context = jnp.einsum(
        "bhqk,bkhd->bqhd", weights_soft, heads_all[2], preferred_element_type=jnp.float32
    )
    context = context.reshape(batch_rows, seq_rows, width_all).astype(jnp.bfloat16)
    after_attn = inputs + jnp.einsum(
        "bld,de->ble", context, frozen_out, preferred_element_type=jnp.float32
    )
    normed_two = layer_norm(after_attn, frozen_gains[1], 0.0).astype(jnp.bfloat16)
    pre_act = jnp.einsum("bld,df->blf", normed_two, frozen_up, preferred_element_type=jnp.float32)
    hidden = jax.nn.gelu(pre_act, approximate=True).astype(jnp.bfloat16)
    outputs = after_attn + jnp.einsum(
        "blf,fd->bld", hidden, frozen_down, preferred_element_type=jnp.float32
    )
    leading = outputs[:, 0, :]
    return (leading * lax.rsqrt(jnp.sum(leading * leading, axis=1, keepdims=True) + 1e-06)).astype(
        jnp.bfloat16
    )


def lamb_parts(weight, grad, first, second, axes):
    mean_new = 0.9 * first + 0.1 * grad
    square_new = 0.999 * second + 0.001 * grad * grad
    update = (
        mean_new / (1.0 - 0.9**STEP) / (jnp.sqrt(square_new / (1.0 - 0.999**STEP)) + 1e-06)
        + weight_decay * weight
    )
    weight_sq = jnp.sum(weight * weight, axis=axes)
    update_sq = jnp.sum(update * update, axis=axes)
    return (update, mean_new, square_new, weight_sq.reshape(-1), update_sq.reshape(-1))


def shards(
    captions,
    token_ids,
    pairing,
    low_images,
    high_images,
    frozen_qkv,
    frozen_out,
    frozen_up,
    frozen_down,
    frozen_gains,
    master_qkv,
    master_out,
    master_up,
    master_down,
    master_norms,
    first_qkv,
    first_out,
    first_up,
    first_down,
    first_norms,
    second_qkv,
    second_out,
    second_up,
    second_down,
    second_norms,
):
    bf16 = jnp.bfloat16
    f32 = jnp.float32
    full_qkv, full_out, full_up, full_down, full_norms = (
        lax.all_gather(master_qkv.astype(bf16), "dp", axis=1, tiled=True),
        lax.all_gather(master_out.astype(bf16), "dp", axis=1, tiled=True),
        lax.all_gather(master_up.astype(bf16), "dp", axis=0, tiled=True),
        lax.all_gather(master_down.astype(bf16), "dp", axis=1, tiled=True),
        lax.all_gather(master_norms.astype(bf16), "dp", axis=1, tiled=True),
    )
    norm_vals = full_norms.astype(f32)
    low_embed = frozen_embed(
        low_images, frozen_qkv, frozen_out, frozen_up, frozen_down, frozen_gains
    )
    high_embed = frozen_embed(
        high_images, frozen_qkv, frozen_out, frozen_up, frozen_down, frozen_gains
    )
    local_images = jnp.concatenate([low_embed, high_embed], axis=0)
    cap_rows, seq_rows, width_all = captions.shape
    local_width = full_qkv.shape[2]
    local_heads = local_width // HEAD_DIM
    head_scale = HEAD_DIM ** (-0.5)
    inputs = captions.astype(f32)
    alive = (token_ids != 0).astype(f32)
    causal = jnp.tril(jnp.ones((seq_rows, seq_rows), dtype=jnp.bool_))
    keep_mask = causal[None, None] & (alive[:, None, None, :] > 0.5)
    normed_one = layer_norm(inputs, norm_vals[0], norm_vals[1]).astype(bf16)
    projected = jnp.einsum(
        "bld,tde->tble", normed_one, full_qkv, preferred_element_type=f32
    ).astype(bf16)
    heads_all = projected.reshape(3, cap_rows, seq_rows, local_heads, HEAD_DIM)
    query_heads, key_heads, value_heads = (heads_all[0], heads_all[1], heads_all[2])
    scores = (
        jnp.einsum("bqhd,bkhd->bhqk", query_heads, key_heads, preferred_element_type=f32)
        * head_scale
    )
    scores = jnp.where(keep_mask, scores, -1e30)
    weights_soft = jax.nn.softmax(scores, axis=-1)
    weights_low = weights_soft.astype(bf16)
    context = jnp.einsum("bhqk,bkhd->bqhd", weights_low, value_heads, preferred_element_type=f32)
    context = context.reshape(cap_rows, seq_rows, local_width).astype(bf16)
    attn_part = jnp.einsum("bld,de->ble", context, full_out, preferred_element_type=f32)
    after_attn = inputs + lax.psum(attn_part, "mp")
    normed_two = layer_norm(after_attn, norm_vals[2], norm_vals[3]).astype(bf16)
    pre_act = jnp.einsum("bld,df->blf", normed_two, full_up, preferred_element_type=f32)
    hidden = jax.nn.gelu(pre_act, approximate=True).astype(bf16)
    mlp_part = jnp.einsum("blf,fd->bld", hidden, full_down, preferred_element_type=f32)
    outputs = after_attn + lax.psum(mlp_part, "mp")
    counted = jnp.sum(alive, axis=1, keepdims=True)
    pooled = jnp.sum(outputs * alive[:, :, None], axis=1) / counted
    inverse = lax.rsqrt(jnp.sum(pooled * pooled, axis=1, keepdims=True) + 1e-06)
    unit = pooled * inverse
    text = unit.astype(bf16)
    images_all = lax.all_gather(local_images, ("dp", "mp"), axis=0, tiled=True)
    total_caps = images_all.shape[0]
    logits = logit_scale * jnp.dot(text, images_all.T, preferred_element_type=f32)
    row_top = jnp.max(logits, axis=1, keepdims=True)
    row_lse = row_top + jnp.log(jnp.sum(jnp.exp(logits - row_top), axis=1, keepdims=True))
    matched = (jnp.arange(total_caps, dtype=jnp.int32)[None, :] == pairing[:, None]).astype(f32)
    dlogits = (jnp.exp(logits - row_lse) - matched) / total_caps
    dscores = (logit_scale * dlogits).astype(bf16)
    dunit = jnp.dot(dscores, images_all, preferred_element_type=f32)
    dpooled = inverse * (dunit - unit * jnp.sum(unit * dunit, axis=1, keepdims=True))
    dout = (dpooled / counted)[:, None, :] * alive[:, :, None]
    dmlp = dout.astype(bf16)
    dhidden = jnp.einsum("bld,fd->blf", dmlp, full_down, preferred_element_type=f32)
    grad_down = jnp.einsum("blf,bld->fd", hidden, dmlp, preferred_element_type=f32)
    gelu_pull = jax.vjp(partial(jax.nn.gelu, approximate=True), pre_act)[1]
    dpre = gelu_pull(dhidden)[0].astype(bf16)
    grad_up = jnp.einsum("bld,blf->df", normed_two, dpre, preferred_element_type=f32)
    dnormed_two = lax.psum(
        jnp.einsum("blf,df->bld", dpre, full_up, preferred_element_type=f32), "mp"
    )
    ln_two_pull = jax.vjp(layer_norm, after_attn, norm_vals[2], norm_vals[3])[1]
    dafter_ln, dgain_two, dshift_two = ln_two_pull(dnormed_two)
    dafter = dout + dafter_ln
    dattn = dafter.astype(bf16)
    grad_out = jnp.einsum("bld,ble->de", context, dattn, preferred_element_type=f32)
    dcontext = jnp.einsum("ble,de->bld", dattn, full_out, preferred_element_type=f32).astype(bf16)
    dcontext = dcontext.reshape(cap_rows, seq_rows, local_heads, HEAD_DIM)
    dweights = jnp.einsum("bqhd,bkhd->bhqk", dcontext, value_heads, preferred_element_type=f32)
    dlogit_attn = weights_soft * (
        dweights - jnp.sum(weights_soft * dweights, axis=-1, keepdims=True)
    )
    dlogit_low = dlogit_attn.astype(bf16)
    dquery = (
        jnp.einsum("bhqk,bkhd->bqhd", dlogit_low, key_heads, preferred_element_type=f32)
        * head_scale
    ).astype(bf16)
    dkey = (
        jnp.einsum("bhqk,bqhd->bkhd", dlogit_low, query_heads, preferred_element_type=f32)
        * head_scale
    ).astype(bf16)
    dvalue = jnp.einsum(
        "bhqk,bqhd->bkhd", weights_low, dcontext, preferred_element_type=f32
    ).astype(bf16)
    dprojected = jnp.stack([dquery, dkey, dvalue]).reshape(3, cap_rows, seq_rows, local_width)
    grad_qkv = jnp.einsum("bld,tble->tde", normed_one, dprojected, preferred_element_type=f32)
    dnormed_one = lax.psum(
        jnp.einsum("tble,tde->bld", dprojected, full_qkv, preferred_element_type=f32), "mp"
    )
    ln_one_pull = jax.vjp(layer_norm, inputs, norm_vals[0], norm_vals[1])[1]
    dinput_ln, dgain_one, dshift_one = ln_one_pull(dnormed_one)
    input_grad = dafter + dinput_ln
    grad_norms_local = jnp.stack([dgain_one, dshift_one, dgain_two, dshift_two])
    local_grads = (grad_qkv, grad_out, grad_up, grad_down, grad_norms_local)
    masters = (master_qkv, master_out, master_up, master_down, master_norms)
    slice_dims = (1, 1, 0, 1, 1)
    summed = lax.psum(
        (local_grads[0], local_grads[1], local_grads[2], local_grads[3], local_grads[4]), "dp"
    )
    dp_index = lax.axis_index("dp")
    shard_grads = tuple(
        (
            lax.dynamic_slice_in_dim(
                summed[index],
                dp_index * masters[index].shape[slice_dims[index]],
                masters[index].shape[slice_dims[index]],
                slice_dims[index],
            )
            for index in range(5)
        )
    )
    firsts = (first_qkv, first_out, first_up, first_down, first_norms)
    seconds = (second_qkv, second_out, second_up, second_down, second_norms)
    axes_all = ((1, 2), (0, 1), (0, 1), (0, 1), (1,))
    parts = [
        lamb_parts(
            masters[index], shard_grads[index], firsts[index], seconds[index], axes_all[index]
        )
        for index in range(5)
    ]
    lead_flag = (lax.axis_index("mp") == 0).astype(f32)
    weight_squares = jnp.concatenate(
        [parts[0][3], parts[1][3], parts[2][3], parts[3][3], parts[4][3] * lead_flag]
    )
    update_squares = jnp.concatenate(
        [parts[0][4], parts[1][4], parts[2][4], parts[3][4], parts[4][4] * lead_flag]
    )
    total_squares = lax.psum(jnp.stack([weight_squares, update_squares]), ("dp", "mp"))
    matrix_norms = jnp.sqrt(total_squares)
    ratios = matrix_norms[0] / matrix_norms[1]
    ratio_pieces = (
        ratios[0:3].reshape(3, 1, 1),
        ratios[3],
        ratios[4],
        ratios[5],
        ratios[6:10].reshape(4, 1),
    )
    news = [
        masters[index] - learning_rate * ratio_pieces[index] * parts[index][0] for index in range(5)
    ]
    copies = [fresh.astype(bf16) for fresh in news]
    return (
        input_grad,
        shard_grads[0],
        shard_grads[1],
        shard_grads[2],
        shard_grads[3],
        shard_grads[4],
        news[0],
        news[1],
        news[2],
        news[3],
        news[4],
        copies[0],
        copies[1],
        copies[2],
        copies[3],
        copies[4],
        parts[0][1],
        parts[1][1],
        parts[2][1],
        parts[3][1],
        parts[4][1],
        parts[0][2],
        parts[1][2],
        parts[2][2],
        parts[3][2],
        parts[4][2],
        matrix_norms,
    )


MESH = pl.DeviceIdType.MESH
BF = jnp.bfloat16
F32 = jnp.float32
HIGHEST = lax.Precision.HIGHEST


def nn(a, b):
    return lax.dot_general(a, b, (((1,), (0,)), ((), ())), preferred_element_type=F32)


def nt(a, b):
    return lax.dot_general(a, b, (((1,), (1,)), ((), ())), preferred_element_type=F32)


def tn(a, b):
    return lax.dot_general(a, b, (((0,), (0,)), ((), ())), preferred_element_type=F32)


def iota(shape, dim):
    return lax.broadcasted_iota(jnp.int32, shape, dim)


def stats(values):
    centre = values - jnp.mean(values, axis=-1, keepdims=True)
    return centre, lax.rsqrt(jnp.mean(centre * centre, axis=-1, keepdims=True) + 1e-05)


def gelu_pair(u):
    root = 0.7978845608028654
    square = u * u
    t = jnp.tanh(root * (u + 0.044715 * square * u))
    half = 0.5 * (1.0 + t)
    slope = half + 0.5 * u * (1.0 - t * t) * (root * (1.0 + 3.0 * 0.044715 * square))
    return u * half, slope


def gelu_only(u):
    root = 0.7978845608028654
    return 0.5 * u * (1.0 + jnp.tanh(root * (u + 0.044715 * u * u * u)))


def pack_attn(qkv_ref, out_ref):
    q, k, v = qkv_ref[0], qkv_ref[1], qkv_ref[2]
    out_t = out_ref[...].T
    return [
        q[:, 0:128],
        k[:, 0:128],
        v[:, 0:128],
        jnp.concatenate([q[:, 128:192], v[:, 128:192]], axis=1),
        jnp.concatenate([k[:, 128:192], out_t[:, 128:192]], axis=1),
        out_t[:, 0:128],
    ]


def lamb_update(weight, grad, first, second):
    mean_new = 0.9 * first + 0.1 * grad
    square_new = 0.999 * second + 0.001 * grad * grad
    update = (
        mean_new * (1.0 / (1.0 - 0.9**STEP))
        / (jnp.sqrt(square_new * (1.0 / (1.0 - 0.999**STEP))) + 1e-06)
        + weight_decay * weight
    )
    return update, mean_new, square_new


CHUNKS = 4


def scratch_table():
    vm = pltpu.VMEM
    dma = pltpu.SemaphoreType.DMA
    return dict(
        cap=vm((1024, 768), BF),
        tok=vm((16, 64), jnp.int32),
        pair=vm((1, 64), jnp.int32),
        alive=vm((8, 128), F32),
        pair_v=vm((64, 1), F32),
        fg_v=vm((2, 768), F32),
        qkv_v=vm((3, 96, 192), F32),
        out_v=vm((192, 96), F32),
        up_v=vm((96, 768), F32),
        down_v=vm((96, 768), F32),
        norms_v=vm((4, 96), F32),
        fin_v=vm((4, 96), F32),
        sen_v=vm((4, 96), F32),
        gsh=vm((3, 96, 768), F32),
        gn=vm((8, 128), F32),
        tot=vm((8, 128), F32),
        w=vm((3, 768, 768), BF),
        ns=vm((16, 128), F32),
        nsend=vm((16, 128), BF),
        nslot=vm((8, 16, 128), BF),
        normp=vm((16, 768), F32),
        mu=vm((1024, 1), F32),
        rs=vm((1024, 1), F32),
        causal=vm((128, 128), F32),
        n1=vm((1024, 768), BF),
        proj=vm((1024, 640), BF),
        p=vm((8, 3, 128, 128), F32),
        o=vm((1024, 256), BF),
        part=vm((1024, 768), F32),
        cs=vm((CHUNKS, 128, 768), BF),
        cr1=vm((CHUNKS, 128, 768), BF),
        cr2=vm((CHUNKS, 128, 768), BF),
        xs=vm((CHUNKS, 128, 768), BF),
        xr1=vm((CHUNKS, 128, 768), BF),
        xr2=vm((CHUNKS, 128, 768), BF),
        a=vm((CHUNKS, 128, 768), F32),
        n2=vm((1024, 768), BF),
        gp=vm((1024, 768), F32),
        hs=vm((2, 32, 768), F32),
        hl=vm((128, 768), BF),
        asum=vm((32, 768), F32),
        cnt=vm((32, 128), F32),
        pp=vm((2, 32, 768), F32),
        pcr=vm((32, 768), F32),
        pxs=vm((32, 768), F32),
        pxr=vm((32, 768), F32),
        emb=vm((4, 2, 4, 16, 768), BF),
        dy=vm((2, 32, 768), BF),
        dpc=vm((32, 768), F32),
        dh=vm((2, 32, 768), F32),
        dz=vm((1024, 768), BF),
        rss=vm((3, 2, 7, 48, 768), BF),
        rsr=vm((3, 2, 7, 48, 768), BF),
        gns=vm((8, 768), F32),
        gnr=vm((8, 768), F32),
        gsl=vm((8, 8, 128), F32),
        gslr=vm((9, 8, 128), F32),
        sqd=vm((8, 8, 128), F32),
        sqm=vm((4, 8, 128), F32),
        loc=dma((15,)),
        first=dma((10,)),
        fin=dma((5,)),
        nsem=dma((8,)),
        ags=dma((3,)),
        agr=dma((3, 2, 7)),
        rsa=dma((3,)),
        rsb=dma((3, 2, 7)),
        arcs=dma((CHUNKS,)),
        arcr=dma((3, CHUNKS)),
        arxs=dma((CHUNKS,)),
        arxr=dma((3, CHUNKS)),
        shs=dma((3,)),
        shr=dma((3, CHUNKS)),
        pos=dma((3,)),
        por=dma((3,)),
        ems=dma((5,)),
        emr=dma((7,)),
        gss=dma((3,)),
        gsr=dma((9,)),
        sqs=dma((2,)),
        sqr=dma((10,)),
        outs=dma((CHUNKS,)),
    )


def step_kernel(names, total_caps, *refs):
    r = SimpleNamespace(**dict(zip(names, refs)))
    dp = lax.axis_index("dp")
    mp = lax.axis_index("mp")
    z, y = dp // 2, dp % 2
    x, c = mp // 2, mp % 2
    sib = (dp, x * 2 + (1 - c))
    xnb = (dp, (1 - x) * 2 + c)
    diag = (dp, (1 - x) * 2 + (1 - c))
    ynb = (z * 2 + (1 - y), mp)
    place_on_ring = z + y * (7 - 2 * z)

    def ring(k):
        q = (place_on_ring + k + 8) % 8
        return (q + (q // 4) * (7 - 2 * q)) * 2 + q // 4

    ways = ((ring(1), mp), (ring(-1), mp))
    zpeer = {k: (((z + k) % 4) * 2 + y, mp) for k in (1, 2, 3)}
    dpeer = {k: ((dp + k) % 8, mp) for k in range(1, 8)}

    def rcopy(src, dst, ssem, rsem, dev):
        return pltpu.make_async_remote_copy(
            src_ref=src, dst_ref=dst, send_sem=ssem, recv_sem=rsem,
            device_id=dev, device_id_type=MESH,
        )

    sends = []

    def go(make, at_end=True):
        copy = make()
        copy.start()
        if at_end:
            sends.append(make)
        return copy

    w = r.w

    def shard_rows(zz, yy):
        return pl.ds(pl.multiple_of((zz * 2 + yy) * 96, 96), 96)

    def own_rows(k):
        return pl.ds(pl.multiple_of(256 * k + 128 * c, 128), 128)

    def sib_rows(k):
        return pl.ds(pl.multiple_of(256 * k + 128 * (1 - c), 128), 128)

    firsts = [
        pltpu.make_async_copy(source, target, r.first.at[n])
        for n, (source, target) in enumerate(
            (
                (r.mq_h, r.qkv_v), (r.mo_h, r.out_v), (r.mn_h, r.norms_v), (r.mu_h, r.up_v),
                (r.md_h, r.down_v), (r.fg_h, r.fg_v), (r.tok_h, r.tok), (r.pair_h, r.pair),
                (r.fin_h, r.fin_v), (r.sen_h, r.sen_v),
            )
        )
    ]
    for copy in firsts:
        copy.start()
    cap_copy = pltpu.make_async_copy(r.cap_h, r.cap, r.loc.at[0])
    cap_copy.start()

    def piece(k, half):
        return pl.ds(pl.multiple_of(ring(k) * 96 + 48 * half, 16), 48)

    def ag_copy(kind, way, step, half, k):
        rows = w.at[kind, piece(k, half)]
        index = min(2 * step + half, 6)
        return rcopy(rows, rows, r.ags.at[kind], r.agr.at[kind, way, index], ways[way])

    def ag_own(kind, way):
        for half in (0, 1):
            go(partial(ag_copy, kind, way, 0, half, 0), False)

    def ag_step(kind, step, half):
        for way in (0, 1):
            if step == 3 and way != half:
                continue
            k = -step if way == 0 else step
            ag_copy(kind, way, step - 1, half, k).wait_recv()
            go(partial(ag_copy, kind, way, step, half, k), False)

    def ag_done(kind):
        ag_copy(kind, 0, 2, 1, -3).wait_recv()
        ag_copy(kind, 1, 2, 0, 3).wait_recv()
        ag_copy(kind, 0, 3, 0, -4).wait_recv()
        ag_copy(kind, 1, 3, 1, 4).wait_recv()

    def core_copy(which, k, received):
        return rcopy(r.cs.at[k], received.at[k], r.arcs.at[k], r.arcr.at[which, k], sib)

    def x_copy(which, k, received_x):
        return rcopy(r.xs.at[k], received_x.at[k], r.arxs.at[k], r.arxr.at[which, k], xnb)

    def ar_start(which, k, received):
        if which > 0:
            core_copy(which - 1, k, received).wait_send()
        r.cs[k] = r.part[sib_rows(k), :].astype(BF)
        go(lambda: core_copy(which, k, received), which == 2)

    def ar_mid(which, k, received, received_x):
        core_copy(which, k, received).wait_recv()
        if which > 0:
            x_copy(which - 1, k, received_x).wait_send()
        r.xs[k] = (r.part[own_rows(k), :] + received[k].astype(F32)).astype(BF)
        go(lambda: x_copy(which, k, received_x), which == 2)

    def ar_end(which, k, received_x):
        x_copy(which, k, received_x).wait_recv()
        return r.xs[k].astype(F32) + received_x[k].astype(F32)

    def share_copy(which, k, ref, rows):
        part = ref.at[rows(k)]
        return rcopy(part, part, r.shs.at[which], r.shr.at[which, k], sib)

    def share(which, k, ref):
        go(lambda: share_copy(which, k, ref, own_rows), False)

    def share_wait(which, k, ref):
        share_copy(which, k, ref, sib_rows).wait_recv()

    barrier = pltpu.get_barrier_semaphore()
    partners = [sib, xnb, diag] + [dpeer[k] for k in range(1, 8)]
    for dev in partners:
        pl.semaphore_signal(barrier, inc=1, device_id=dev, device_id_type=MESH)
    for copy in firsts[0:3]:
        copy.wait()
    tiles = pack_attn(r.qkv_v, r.out_v)
    mine = shard_rows(z, y)
    for t in range(6):
        w[0, mine, 128 * t : 128 * (t + 1)] = tiles[t].astype(BF)
    r.ns[...] = jnp.zeros((16, 128), F32)
    r.ns[0:4, 0:96] = r.norms_v[...]
    r.nsend[...] = r.ns[...].astype(BF)
    r.nslot[dp] = r.nsend[...]

    pl.semaphore_wait(barrier, len(partners))

    def norm_copy(k, source):
        return rcopy(
            r.nsend, r.nslot.at[source()], r.nsem.at[7], r.nsem.at[k - 1], dpeer[k]
        )

    for k in range(1, 8):
        go(partial(norm_copy, k, lambda: dp), False)
    for way in (0, 1):
        ag_own(0, way)
    for copy in firsts[3:10]:
        copy.wait()
    w[1, mine, :] = r.up_v[...].astype(BF)
    w[2, mine, :] = r.down_v[...].astype(BF)

    live = jnp.where(r.tok[...] != 0, 1.0, 0.0).astype(BF)
    spread_caps = jnp.where(iota((64, 1024), 1) // 16 == iota((64, 1024), 0), 1.0, 0.0).astype(BF)
    live_all = nn(live, spread_caps)
    live_row = jnp.sum(
        jnp.where(iota((16, 1024), 1) % 16 == iota((16, 1024), 0), live_all, 0.0), axis=0, keepdims=True
    )
    for b in range(8):
        r.alive[b : b + 1, :] = live_row[:, 128 * b : 128 * (b + 1)]
    image = r.pair[...]
    owner_dp = image // 64
    column = ((((image // 16) % 4) * 2 + owner_dp % 2) * 4 + owner_dp // 2) * 16 + image % 16
    order = iota((64, 64), 0)
    caption = 16 * ((order % 32) // 8) + 8 * (order // 32) + order % 8
    r.pair_v[...] = jnp.sum(
        jnp.where(iota((64, 64), 1) == caption, column.astype(F32), 0.0), axis=1, keepdims=True
    )

    rows_i = iota((128, 128), 0)
    lanes_i = iota((128, 128), 1)
    r.causal[...] = jnp.where(
        (rows_i // 16 == lanes_i // 16) & (lanes_i <= rows_i), 1.0, 0.0
    ).astype(F32)

    def emb_copy(index, dev, pick):
        ref = pick()
        return rcopy(ref, ref, r.ems.at[max(index - 2, 0)], r.emr.at[index], dev)

    def image_phase(iq, io, iu, idn, low, high, qt, pn, x0, lows):
        copies = [
            pltpu.make_async_copy(r.fqkv_h, iq, r.loc.at[1]),
            pltpu.make_async_copy(r.high_h, high, r.loc.at[2]),
            pltpu.make_async_copy(r.low_h, low, r.loc.at[3]),
            pltpu.make_async_copy(r.fout_h, io, r.loc.at[4]),
            pltpu.make_async_copy(r.fup_h, iu, r.loc.at[5]),
            pltpu.make_async_copy(r.fdown_h, idn, r.loc.at[6]),
        ]
        for copy in copies:
            copy.start()
        copies[1].wait()
        copies[2].wait()
        g1 = r.fg_v[0:1, :]
        g2 = r.fg_v[1:2, :]
        x0[0:2, :] = low[0].astype(F32)
        for n in range(50):
            lows[2 * n : 2 * n + 2, :] = low[n].astype(F32)
        for b in range(14):
            x0[b + 2 : b + 3, :] = high[b, 0:1, :].astype(F32)
        centre, inv = stats(x0[...])
        first = (centre * inv * g1).astype(BF)
        copies[0].wait()
        query = nn(first, iq[0]).astype(BF).astype(F32) * 0.125
        head = iota((16, 768), 1) // 64 == iota((16, 768), 0)
        spread = jnp.concatenate(
            [jnp.where(head, query[b : b + 1, :], 0.0).astype(BF) for b in range(16)], axis=0
        )
        qt[...] = nt(spread, iq[1]).astype(BF)

        def attend(rows, slot, keep=None):
            centre, inv = stats(rows)
            normed = (centre * inv * g1).astype(BF)
            at = pl.ds(pl.multiple_of(slot * 16, 16), 16)
            scores = nt(qt[at, :], normed)
            if keep is not None:
                scores = jnp.where(keep, scores, -1e30)
            e = jnp.exp(scores - jnp.max(scores, axis=-1, keepdims=True))
            soft = (e / jnp.sum(e, axis=-1, keepdims=True)).astype(BF)
            pn[at, :] = nn(soft, normed).astype(BF)

        for b in range(2):
            attend(lows[...], b, iota((16, 100), 1) % 2 == b)

        def some(b, carry):
            attend(high[b].astype(F32), b + 2)
            return carry

        ag_step(0, 1, 0)
        lax.fori_loop(0, 2, some, 0)
        ag_step(0, 1, 1)
        lax.fori_loop(2, 5, some, 0)
        ag_step(0, 2, 0)
        lax.fori_loop(5, 7, some, 0)
        ag_step(0, 2, 1)
        lax.fori_loop(7, 10, some, 0)
        ag_step(0, 3, 0)
        ag_own(1, 0)
        text_norm()
        ag_step(0, 3, 1)
        ag_own(1, 1)
        lax.fori_loop(10, 13, some, 0)
        ag_done(0)
        attention_forward(0)
        ag_step(1, 1, 0)
        attention_forward(1)
        ar_mid(0, 0, r.cr1, r.xr1)
        ag_step(1, 1, 1)
        attention_forward(2)
        ar_mid(0, 1, r.cr1, r.xr1)
        ag_step(1, 2, 0)
        attention_forward(3)
        ar_mid(0, 2, r.cr1, r.xr1)
        ag_step(1, 2, 1)
        lax.fori_loop(13, 14, some, 0)
        ar_mid(0, 3, r.cr1, r.xr1)
        values = nn(pn[...], iq[2])
        head_all = iota((256, 768), 1) // 64 == iota((256, 768), 0) % 16
        picked = jnp.where(head_all, values, 0.0).astype(BF)
        chooser = jnp.where(iota((16, 256), 1) // 16 == iota((16, 256), 0), 1.0, 0.0).astype(BF)
        context = nn(chooser, picked).astype(BF)
        copies[3].wait()
        after = x0[...] + nn(context, io[...])
        centre, inv = stats(after)
        second = (centre * inv * g2).astype(BF)
        ag_step(1, 3, 0)
        ag_own(2, 0)
        copies[4].wait()
        copies[5].wait()
        leading = after
        for t in range(4):
            cols = slice(768 * t, 768 * (t + 1))
            hidden = gelu_only(nn(second, iu[:, cols])).astype(BF)
            leading = leading + nn(hidden, idn[cols, :])
        norm = lax.rsqrt(jnp.sum(leading * leading, axis=1, keepdims=True) + 1e-06)
        r.emb[mp, y, z] = (leading * norm).astype(BF)
        for k in (1, 2, 3):
            go(partial(emb_copy, k - 1, zpeer[k], lambda: r.emb.at[mp, y, z]), False)

    def emb_y():
        for k in (1, 2, 3):
            emb_copy(k - 1, zpeer[k], lambda: r.emb.at[mp, y, (z - k + 4) % 4]).wait_recv()
        go(lambda: emb_copy(3, ynb, lambda: r.emb.at[mp, y]))

    def emb_x():
        emb_copy(3, ynb, lambda: r.emb.at[mp, 1 - y]).wait_recv()
        go(lambda: emb_copy(4, xnb, lambda: r.emb.at[mp]))
        go(lambda: emb_copy(5, sib, lambda: r.emb.at[mp]))

    def emb_c():
        emb_copy(4, xnb, lambda: r.emb.at[(1 - x) * 2 + c]).wait_recv()
        go(lambda: emb_copy(6, sib, lambda: r.emb.at[(1 - x) * 2 + c]))

    def emb_done():
        emb_copy(5, sib, lambda: r.emb.at[x * 2 + 1 - c]).wait_recv()
        emb_copy(6, sib, lambda: r.emb.at[(1 - x) * 2 + 1 - c]).wait_recv()

    def text_norm():
        for k in range(1, 8):
            norm_copy(k, lambda: (dp - k + 8) % 8).wait_recv()
        place_r = iota((1024, 768), 0)
        place = jnp.where(
            (iota((1024, 768), 1) == (place_r // 128) * 96 + place_r % 128) & (place_r % 128 < 96), 1.0, 0.0
        ).astype(BF)
        r.normp[...] = nn(jnp.concatenate([r.nslot[i] for i in range(8)], axis=1), place)
        cap_copy.wait()
        for k in range(CHUNKS):
            rows = slice(256 * k, 256 * (k + 1))
            values = r.cap[rows, :].astype(F32)
            mu = jnp.mean(values, axis=-1, keepdims=True)
            centre = values - mu
            inv = lax.rsqrt(jnp.mean(centre * centre, axis=-1, keepdims=True) + 1e-05)
            r.mu[rows, :] = mu
            r.rs[rows, :] = inv
            r.n1[rows, :] = (centre * inv * r.normp[0:1, :] + r.normp[1:2, :]).astype(BF)

    lane = iota((1, 128), 1)
    lo = jnp.where(lane < 64, 1.0, 0.0).astype(BF)
    hi = jnp.where(lane < 64, 0.0, 1.0).astype(BF)
    is_lo = iota((128, 128), 1) < 64

    def attention_forward(k):
        rows = slice(256 * k, 256 * (k + 1))
        r.proj[rows, :] = nn(r.n1[rows, :], w[0, :, 0:640]).astype(BF)
        for b in (2 * k, 2 * k + 1):
            at = slice(128 * b, 128 * (b + 1))
            t = [r.proj[at, 128 * i : 128 * (i + 1)] for i in range(5)]
            keep = (r.causal[...] * r.alive[b : b + 1, :]) > 0.5
            probs = []
            for h, (left, right) in enumerate(((t[0] * lo, t[1]), (t[0] * hi, t[1]), (t[3] * lo, t[4]))):
                s = jnp.where(keep, nt(left, right) * 0.125, -1e30)
                e = jnp.exp(s - jnp.max(s, axis=-1, keepdims=True))
                p = e * (1.0 / jnp.sum(e, axis=-1, keepdims=True))
                r.p[b, h] = p
                probs.append(p.astype(BF))
            pair = nn(
                jnp.concatenate([probs[0], probs[1]], axis=1),
                jnp.concatenate([t[2] * lo, t[2] * hi], axis=0),
            )
            r.o[at, 0:128] = nn(probs[2], t[3] * hi).astype(BF)
            r.o[at, 128:256] = pair.astype(BF)
        r.part[rows, :] = nt(r.o[rows, :], w[0, :, 512:768])
        ar_start(0, k, r.cr1)

    def own_alive(k):
        row = r.alive[pl.ds(2 * k + c, 1), :]
        return jnp.where(iota((8, 128), 1) // 16 == iota((8, 128), 0), row, 0.0)

    def chunk_alive(k):
        row = jnp.concatenate([r.alive[2 * k : 2 * k + 1, :], r.alive[2 * k + 1 : 2 * k + 2, :]], axis=1)
        return jnp.where(iota((16, 256), 1) // 16 == iota((16, 256), 0), row, 0.0).astype(BF)

    def second_norm(k):
        a = r.cap[own_rows(k), :].astype(F32) + ar_end(0, k, r.xr1)
        r.a[k] = a
        centre, inv = stats(a)
        r.n2[own_rows(k), :] = (centre * inv * r.normp[2:3, :] + r.normp[3:4, :]).astype(BF)
        share(0, k, r.n2)
        alive = own_alive(k)
        at = slice(8 * k, 8 * (k + 1))
        r.asum[at, :] = jnp.dot(alive, a, precision=HIGHEST, preferred_element_type=F32)
        r.cnt[at, :] = jnp.broadcast_to(jnp.sum(alive, axis=1, keepdims=True), (8, 128))

    def mlp_up(k):
        rows = slice(256 * k, 256 * (k + 1))
        share_wait(0, k, r.n2)
        value, slope = gelu_pair(nn(r.n2[rows, :], w[1]))
        r.gp[rows, :] = slope
        sums = nn(chunk_alive(k), value.astype(BF))
        r.hs[0, 8 * k : 8 * (k + 1), :] = sums[0:8]
        r.hs[1, 8 * k : 8 * (k + 1), :] = sums[8:16]

    pl.run_scoped(
        image_phase,
        pltpu.VMEM((3, 768, 768), BF),
        pltpu.VMEM((768, 768), BF),
        pltpu.VMEM((768, 3072), BF),
        pltpu.VMEM((3072, 768), BF),
        pltpu.VMEM((50, 2, 768), BF),
        pltpu.VMEM((14, 145, 768), BF),
        pltpu.VMEM((256, 768), BF),
        pltpu.VMEM((256, 768), BF),
        pltpu.VMEM((16, 768), F32),
        pltpu.VMEM((100, 768), F32),
    )

    ag_step(1, 3, 1)
    ag_own(2, 1)
    second_norm(0)
    ag_done(1)
    ag_step(2, 1, 0)
    mlp_up(0)
    second_norm(1)
    ag_step(2, 1, 1)
    emb_y()
    mlp_up(1)
    ag_step(2, 2, 0)
    second_norm(2)
    ag_step(2, 2, 1)
    emb_x()
    mlp_up(2)
    ag_step(2, 3, 0)
    second_norm(3)
    ag_step(2, 3, 1)
    emb_c()
    mlp_up(3)

    hsum = r.hs[...].reshape(64, 768)
    high_part = hsum.astype(BF)
    r.hl[0:64, :] = high_part
    r.hl[64:128, :] = (hsum - high_part.astype(F32)).astype(BF)
    ag_done(2)
    both = nt(r.hl[...], w[2])
    r.pp[...] = (both[0:64] + both[64:128]).reshape(2, 32, 768)
    first_copy = go(lambda: rcopy(r.pp.at[1 - c], r.pcr, r.pos.at[0], r.por.at[0], sib))
    emb_done()
    first_copy.wait_recv()
    r.pxs[...] = r.pp[c] + r.pcr[...]
    second_copy = go(lambda: rcopy(r.pxs, r.pxr, r.pos.at[1], r.por.at[1], xnb))
    count = r.cnt[:, 0:1]
    second_copy.wait_recv()
    pooled = (r.asum[...] + (r.pxs[...] + r.pxr[...])) / count
    inverse = lax.rsqrt(jnp.sum(pooled * pooled, axis=1, keepdims=True) + 1e-06)
    unit = pooled * inverse
    images = r.emb[...].reshape(total_caps, 768)
    logits = logit_scale * nt(unit.astype(BF), images)
    top = jnp.max(logits, axis=1, keepdims=True)
    row_lse = top + jnp.log(jnp.sum(jnp.exp(logits - top), axis=1, keepdims=True))
    match = iota((32, total_caps), 1).astype(F32) == r.pair_v[pl.ds(pl.multiple_of(32 * c, 32), 32), :]
    dlogits = (jnp.exp(logits - row_lse) - jnp.where(match, 1.0, 0.0)) / total_caps
    dunit = nn((logit_scale * dlogits).astype(BF), images)
    dpooled = inverse * (dunit - unit * jnp.sum(unit * dunit, axis=1, keepdims=True))
    dpc = dpooled / count
    r.dpc[...] = dpc
    r.dy[c] = dpc.astype(BF)

    def dy_copy(core):
        ref = r.dy.at[core]
        return rcopy(ref, ref, r.pos.at[2], r.por.at[2], sib)

    go(lambda: dy_copy(c))

    def backward(du, dpack, g, packed, raw):
        moments = ((r.fiq_h, r.fio_h, r.fiu_h, r.fid_h), (r.seq_h, r.seo_h, r.seu_h, r.sed_h))
        raw_copies = []
        for m in range(2):
            for n in range(4):
                copy = pltpu.make_async_copy(moments[m][n], raw[4 * m + n], r.loc.at[7 + 4 * m + n])
                copy.start()
                raw_copies.append(copy)

        def mlp_backward(k):
            rows = slice(256 * k, 256 * (k + 1))
            dh = jnp.concatenate(
                [r.dh[0, 8 * k : 8 * (k + 1), :], r.dh[1, 8 * k : 8 * (k + 1), :]], axis=0
            )
            dh_high = dh.astype(BF)
            dh_low = (dh - dh_high.astype(F32)).astype(BF)
            alive = chunk_alive(k)
            spread = tn(jnp.concatenate([alive, alive], axis=0), jnp.concatenate([dh_high, dh_low], axis=0))
            value = (r.gp[rows, :] * spread).astype(BF)
            du[rows, :] = value
            r.part[rows, :] = nt(value, w[1])
            ar_start(1, k, r.cr2)

        def rs_copy(kind, way, index):
            return rcopy(
                r.rss.at[kind, way, index], r.rsr.at[kind, way, index],
                r.rsa.at[kind], r.rsb.at[kind, way, index], ways[way],
            )

        def rs_index(step, half):
            return 0 if step == 0 else 2 * step - 1 + half

        def rs_send(kind, way, step, half, add):
            k = 4 - step if way == 0 else step - 4
            value = g[kind, piece(k, half), :]
            if add:
                before = rs_index(step - 1, half)
                rs_copy(kind, way, before).wait_recv()
                value = value + r.rsr[kind, way, before].astype(F32)
            index = rs_index(step, half)
            r.rss[kind, way, index] = value.astype(BF)
            go(partial(rs_copy, kind, way, index), False)

        def rs_start(kind):
            for way in (0, 1):
                rs_send(kind, way, 0, way, False)
            for way in (0, 1):
                rs_send(kind, way, 1, 1 - way, False)

        def rs_step(kind, step, early):
            for way in (0, 1):
                rs_send(kind, way, step, 1 - way if early else way, True)

        def rs_end(kind):
            for half in (0, 1):
                index = rs_index(3, half)
                for way in (0, 1):
                    rs_copy(kind, way, index).wait_recv()
                r.gsh[kind, 48 * half : 48 * half + 48, :] = g[kind, piece(0, half), :] + (
                    r.rsr[kind, 0, index].astype(F32) + r.rsr[kind, 1, index].astype(F32)
                )

        def second_backward(k, dgain, dshift):
            dn = ar_end(1, k, r.xr2)
            centre, inv = stats(r.a[k])
            hat = centre * inv
            dhat = dn * r.normp[2:3, :]
            dln = inv * (
                dhat - jnp.mean(dhat, axis=-1, keepdims=True)
                - hat * jnp.mean(dhat * hat, axis=-1, keepdims=True)
            )
            dout = lax.dot_general(
                own_alive(k), r.dpc[8 * k : 8 * (k + 1), :], (((0,), (0,)), ((), ())),
                precision=HIGHEST, preferred_element_type=F32,
            )
            da = dout + dln
            r.a[k] = da
            r.dz[own_rows(k), :] = da.astype(BF)
            share(1, k, r.dz)
            return (
                dgain + jnp.sum(dn * hat, axis=0, keepdims=True),
                dshift + jnp.sum(dn, axis=0, keepdims=True),
            )

        def attention_backward(k, dgain, dshift):
            rows = slice(256 * k, 256 * (k + 1))
            share_wait(1, k, r.dz)
            do_all = nn(r.dz[rows, :], w[0, :, 512:768]).astype(BF)
            for i, b in enumerate((2 * k, 2 * k + 1)):
                at = slice(128 * b, 128 * (b + 1))
                t = [r.proj[at, 128 * j : 128 * (j + 1)] for j in range(5)]
                do2 = do_all[128 * i : 128 * (i + 1), 0:128] * hi
                do01 = do_all[128 * i : 128 * (i + 1), 128:256]
                ds, ps = [], []
                for h, (left, right) in enumerate(((do01 * lo, t[2]), (do01 * hi, t[2]), (do2, t[3]))):
                    dw = nt(left, right)
                    p = r.p[b, h]
                    ps.append(p.astype(BF))
                    ds.append((p * (dw - jnp.sum(p * dw, axis=-1, keepdims=True))).astype(BF))
                dq = nn(
                    jnp.concatenate([ds[0], ds[1]], axis=1),
                    jnp.concatenate([t[1] * lo, t[1] * hi], axis=0),
                )
                dk = tn(
                    jnp.concatenate([ds[0], ds[1]], axis=0),
                    jnp.concatenate([t[0] * lo, t[0] * hi], axis=0),
                )
                dv = tn(
                    jnp.concatenate([ps[0], ps[1]], axis=0),
                    jnp.concatenate([do01 * lo, do01 * hi], axis=0),
                )
                dq2 = nn(ds[2], t[4] * lo)
                dk2 = tn(ds[2], t[3] * lo)
                dv2 = tn(ps[2], do2)
                dpack[at, 0:128] = (dq * 0.125).astype(BF)
                dpack[at, 128:256] = (dk * 0.125).astype(BF)
                dpack[at, 256:384] = dv.astype(BF)
                dpack[at, 384:512] = (dq2 * 0.125 + dv2).astype(BF)
                dpack[at, 512:640] = (dk2 * 0.125).astype(BF)
            part = nt(dpack[rows, :], w[0, :, 0:640])
            r.part[rows, :] = part
            ar_start(2, k, r.cr1)
            inner = tn(r.n1[rows, :], dpack[rows, :])
            outer = tn(r.dz[rows, :], r.o[rows, :])
            if k == 0:
                g[0, :, 0:512] = inner[:, 0:512]
                g[0, :, 512:640] = inner[:, 512:640] + outer[:, 0:128]
                g[0, :, 640:768] = outer[:, 128:256]
            else:
                g[0, :, 0:512] += inner[:, 0:512]
                g[0, :, 512:640] += inner[:, 512:640] + outer[:, 0:128]
                g[0, :, 640:768] += outer[:, 128:256]
            hat = (r.cap[rows, :].astype(F32) - r.mu[rows, :]) * r.rs[rows, :]
            return (
                dgain + jnp.sum(part * hat, axis=0, keepdims=True),
                dshift + jnp.sum(part, axis=0, keepdims=True),
            )

        dy_copy(1 - c).wait_recv()
        dy = r.dy[...].reshape(64, 768)
        g[2] = tn(jnp.concatenate([dy, dy], axis=0), r.hl[...])
        rs_start(2)
        r.dh[...] = nn(dy, w[2]).reshape(2, 32, 768)

        mlp_backward(0)
        mlp_backward(1)
        ar_mid(1, 0, r.cr2, r.xr2)
        rs_step(2, 1, False)
        mlp_backward(2)
        ar_mid(1, 1, r.cr2, r.xr2)
        rs_step(2, 2, True)
        mlp_backward(3)
        ar_mid(1, 2, r.cr2, r.xr2)
        rs_step(2, 2, False)
        ar_mid(1, 3, r.cr2, r.xr2)
        g[1] = tn(r.n2[...], du[...])
        rs_start(1)
        rs_step(2, 3, True)
        zero = jnp.zeros((1, 768), F32)
        dg2, db2, dg1, db1 = zero, zero, zero, zero
        dg2, db2 = second_backward(0, dg2, db2)
        rs_step(2, 3, False)
        dg1, db1 = attention_backward(0, dg1, db1)
        dg2, db2 = second_backward(1, dg2, db2)
        ar_mid(2, 0, r.cr1, r.xr1)
        rs_step(1, 1, False)
        rs_end(2)
        dg1, db1 = attention_backward(1, dg1, db1)
        rs_step(1, 2, True)
        dg2, db2 = second_backward(2, dg2, db2)
        ar_mid(2, 1, r.cr1, r.xr1)
        rs_step(1, 2, False)
        dg1, db1 = attention_backward(2, dg1, db1)
        rs_step(1, 3, True)
        dg2, db2 = second_backward(3, dg2, db2)
        ar_mid(2, 2, r.cr1, r.xr1)
        rs_step(1, 3, False)
        dg1, db1 = attention_backward(3, dg1, db1)
        rs_start(0)
        ar_mid(2, 3, r.cr1, r.xr1)

        def gn_core():
            return rcopy(r.gns, r.gnr, r.gss.at[0], r.gsr.at[7], sib)

        def gn_slice(k):
            return rcopy(r.gsl.at[(dp + k) % 8], r.gslr.at[k - 1], r.gss.at[1], r.gsr.at[k - 1], dpeer[k])

        def gn_x():
            return rcopy(r.gslr.at[7], r.gslr.at[8], r.gss.at[2], r.gsr.at[8], xnb)

        r.gns[...] = jnp.concatenate(
            [dg1, db1, 0.5 * dg2, 0.5 * db2, jnp.zeros((4, 768), F32)], axis=0
        )
        go(gn_core)

        def out_copy(k, rows):
            return rcopy(
                r.a.at[k], r.ig_o.at[rows(k)], r.shs.at[2], r.shr.at[2, k], sib
            )

        def finish_rows(k):
            dn = ar_end(2, k, r.xr1)
            hat = (r.cap[own_rows(k), :].astype(F32) - r.mu[own_rows(k), :]) * r.rs[own_rows(k), :]
            dhat = dn * r.normp[0:1, :]
            dln = r.rs[own_rows(k), :] * (
                dhat - jnp.mean(dhat, axis=-1, keepdims=True)
                - hat * jnp.mean(dhat * hat, axis=-1, keepdims=True)
            )
            r.a[k] = r.a[k] + dln
            local = pltpu.make_async_copy(r.a.at[k], r.ig_o.at[own_rows(k)], r.outs.at[k])
            local.start()
            go(lambda: out_copy(k, own_rows), False)
            return local

        for t, tile in enumerate(tiles):
            packed[0, 0, :, 128 * t : 128 * (t + 1)] = tile
        packed[0, 1] = r.up_v[...]
        packed[0, 2] = r.down_v[...]
        for copy in raw_copies:
            copy.wait()
        for m in range(2):
            for t, tile in enumerate(pack_attn(raw[4 * m], raw[4 * m + 1])):
                packed[1 + m, 0, :, 128 * t : 128 * (t + 1)] = tile
            packed[1 + m, 1] = raw[4 * m + 2][...]
            packed[1 + m, 2] = raw[4 * m + 3][...]

        gn_core().wait_recv()
        gn_pad = jnp.concatenate([r.gns[...] + r.gnr[...], jnp.zeros((8, 128), F32)], axis=1)
        for i in range(8):
            r.gsl[i] = gn_pad[:, 96 * i : 96 * i + 128]
        for k in range(1, 8):
            go(partial(gn_slice, k), False)
        rs_step(0, 1, False)
        locals_out = [finish_rows(0)]
        rs_step(0, 2, True)
        locals_out.append(finish_rows(1))
        rs_end(1)
        rs_step(0, 2, False)
        gn_mine = r.gsl[dp]
        for k in range(1, 8):
            gn_slice(k).wait_recv()
            gn_mine = gn_mine + r.gslr[k - 1]
        r.gslr[7] = gn_mine
        go(gn_x)
        locals_out.append(finish_rows(2))
        rs_step(0, 3, True)
        locals_out.append(finish_rows(3))
        rs_step(0, 3, False)
        gn_x().wait_recv()
        gn_mine = jnp.where(iota((8, 128), 1) < 96, gn_mine + r.gslr[8], 0.0)
        r.gn[...] = gn_mine
        finals = [pltpu.make_async_copy(r.gn, r.gn_o, r.fin.at[3])]
        finals[0].start()

        sel_lane = iota((8, 128), 1)
        sel_row = iota((8, 128), 0)
        squares = jnp.zeros((8, 128), F32)

        def put(acc, row, index, value):
            return acc + jnp.where((sel_row == row) & (sel_lane == index), value, 0.0)

        quarter = 0.25
        zeros4 = jnp.zeros((4, 96), F32)
        gn4 = gn_mine[0:4, 0:96]
        norm_update, _, _ = lamb_update(r.norms_v[...], gn4, r.fin_v[...], r.sen_v[...])
        for row, value in ((0, r.norms_v[...]), (1, norm_update)):
            line = quarter * jnp.sum(value * value, axis=1, keepdims=True)
            for n in range(4):
                squares = put(squares, row, 6 + n, line[n : n + 1, :])
        lane_all = iota((1, 768), 1)
        third = (lane_all // 64) % 12
        owner = jnp.where(
            lane_all < 384, lane_all // 128,
            jnp.where(
                lane_all < 512, jnp.where(lane_all < 448, 0, 2),
                jnp.where(lane_all < 576, 1, 3),
            ),
        )
        for kind in (2, 1, 0):
            if kind == 0:
                rs_end(0)
            final = pltpu.make_async_copy(r.gsh.at[kind], r.gsh_o.at[kind], r.fin.at[kind])
            final.start()
            finals.append(final)
            update, _, _ = lamb_update(packed[0, kind], r.gsh[kind], packed[1, kind], packed[2, kind])
            for row, value in ((0, packed[0, kind]), (1, update)):
                line = jnp.sum(value * value, axis=0, keepdims=True)
                if kind == 0:
                    for n in range(4):
                        part = jnp.sum(jnp.where(owner == n, line, 0.0), axis=1, keepdims=True)
                        squares = put(squares, row, n, part)
                else:
                    squares = put(squares, row, 3 + kind, jnp.sum(line, axis=1, keepdims=True))

        sqd, sqm = r.sqd, r.sqm

        def sq_copy(buffer, slot, index, dev):
            ref = buffer.at[slot()]
            return rcopy(ref, ref, r.sqs.at[index // 7], r.sqr.at[index], dev)

        sqd[dp] = squares
        for k in range(1, 8):
            go(partial(sq_copy, sqd, lambda: dp, k - 1, dpeer[k]), False)
        for k in range(1, 8):
            sq_copy(sqd, lambda: (dp - k + 8) % 8, k - 1, dpeer[k]).wait_recv()
        total = sqd[0]
        for i in range(1, 8):
            total = total + sqd[i]
        sqm[mp] = total
        others = ((sib, x * 2 + 1 - c), (xnb, (1 - x) * 2 + c), (diag, (1 - x) * 2 + 1 - c))
        for n, (dev, _) in enumerate(others):
            go(partial(sq_copy, sqm, lambda: mp, 7 + n, dev), False)
        for n, (dev, source) in enumerate(others):
            sq_copy(sqm, lambda: source, 7 + n, dev).wait_recv()
        r.tot[...] = (sqm[0] + sqm[1]) + (sqm[2] + sqm[3])
        final = pltpu.make_async_copy(r.tot, r.tot_o, r.fin.at[4])
        final.start()
        finals.append(final)
        for local in locals_out + finals:
            local.wait()
        for k in range(CHUNKS):
            out_copy(k, sib_rows).wait_recv()

    pl.run_scoped(
        backward,
        pltpu.VMEM((1024, 768), BF),
        pltpu.VMEM((1024, 640), BF),
        pltpu.VMEM((3, 768, 768), F32),
        pltpu.VMEM((3, 3, 96, 768), F32),
        [
            pltpu.VMEM(shape, F32)
            for _ in range(2)
            for shape in ((3, 96, 192), (192, 96), (96, 768), (96, 768))
        ],
    )
    for make in sends:
        make().wait_send()

    def all_sent(ref, sem):
        rcopy(ref, ref, sem, sem, sib).wait_send()

    all_sent(r.nslot.at[pl.ds(0, 7)], r.nsem.at[7])
    for kind in range(3):
        all_sent(w.at[kind, pl.ds(0, 672)], r.ags.at[kind])
        all_sent(r.rss.at[kind], r.rsa.at[kind])
    all_sent(r.n2.at[pl.ds(0, 512)], r.shs.at[0])
    all_sent(r.dz.at[pl.ds(0, 512)], r.shs.at[1])
    all_sent(r.a, r.shs.at[2])
    all_sent(r.emb.at[0, 0, pl.ds(0, 3)], r.ems.at[0])
    all_sent(r.gslr.at[pl.ds(0, 7)], r.gss.at[1])
    all_sent(r.sqd.at[pl.ds(0, 7)], r.sqs.at[0])
    all_sent(r.sqm.at[pl.ds(0, 3)], r.sqs.at[1])


def lamb_kernel(*refs):
    sources, targets = refs[0:19], refs[19:46]
    buffers, results = refs[46:64], refs[64:90]
    rows, in_sem, out_sem = refs[90:93]
    pieces = []
    for n in range(4):
        at = pl.ds(256 * n, 256)
        pieces.append(
            (
                pltpu.make_async_copy(sources[18].at[at], rows.at[at], in_sem.at[18 + n]),
                pltpu.make_async_copy(rows.at[at], targets[26].at[at], out_sem.at[26 + n]),
            )
        )
    loads = [pltpu.make_async_copy(sources[n], buffers[n], in_sem.at[n]) for n in range(18)]
    for copy in loads:
        copy.start()
    for load, _ in pieces:
        load.start()
    stores = []
    (gsh, gn, tot, w_qkv, w_out, w_up, w_down, w_norms, m_qkv, m_out, m_up, m_down, m_norms,
     v_qkv, v_out, v_up, v_down, v_norms) = buffers
    grads, news, copies, means, squares = (results[5 * i : 5 * i + 5] for i in range(5))

    def store(n):
        copy = pltpu.make_async_copy(results[n], targets[n], out_sem.at[n])
        copy.start()
        stores.append(copy)

    def ready(*which):
        for n in which:
            loads[n].wait()

    def rows_through(n):
        pieces[n][0].wait()
        pieces[n][1].start()
        stores.append(pieces[n][1])

    ready(0, 1, 2, 5, 10, 15)
    roots = jnp.sqrt(tot[0:2, :])
    results[25][...] = roots[:, 0:10]
    store(25)
    ratio = learning_rate * (roots[0:1, :] / roots[1:2, :])

    def one(index, at, scale, grad, weight, first, second):
        update, mean_new, square_new = lamb_update(weight, grad, first, second)
        fresh = weight - scale * update
        for group, value in zip(
            (grads, news, copies, means, squares), (grad, fresh, fresh.astype(BF), mean_new, square_new)
        ):
            group[index][at] = value

    def send(index):
        for group in range(5):
            store(5 * group + index)

    one(2, Ellipsis, ratio[:, 4:5], gsh[1], w_up[...], m_up[...], v_up[...])
    send(2)
    ready(6, 11, 16)
    one(3, Ellipsis, ratio[:, 5:6], gsh[2], w_down[...], m_down[...], v_down[...])
    send(3)
    ready(3, 8, 13)
    attn = gsh[0]
    third = attn[:, 384:512]
    fourth = attn[:, 512:640]
    parts = (
        jnp.concatenate([attn[:, 0:128], third[:, 0:64]], axis=1),
        jnp.concatenate([attn[:, 128:256], fourth[:, 0:64]], axis=1),
        jnp.concatenate([attn[:, 256:384], third[:, 64:128]], axis=1),
    )
    for n in range(3):
        one(0, n, ratio[:, n : n + 1], parts[n], w_qkv[n], m_qkv[n], v_qkv[n])
    send(0)
    rows_through(0)
    rows_through(1)
    ready(4, 9, 14)
    out_grad = jnp.concatenate([attn[:, 640:768], fourth[:, 64:128]], axis=1).T
    one(1, Ellipsis, ratio[:, 3:4], out_grad, w_out[...], m_out[...], v_out[...])
    send(1)
    rows_through(2)
    rows_through(3)
    ready(7, 12, 17)
    for n in range(4):
        at = (slice(n, n + 1), slice(None))
        one(4, at, ratio[:, 6 + n : 7 + n], gn[n : n + 1, 0:96], w_norms[at], m_norms[at], v_norms[at])
    send(4)
    for copy in stores:
        copy.wait()


def fused_shards(
    captions, token_ids, pairing, low_images, high_images, frozen_qkv, frozen_out, frozen_up,
    frozen_down, frozen_gains, *state
):
    masters, firsts, seconds = state[0:5], state[5:10], state[10:15]
    cap_rows, seq_rows, width_all = captions.shape
    rows = cap_rows * seq_rows
    total_caps = cap_rows * lax.axis_size("dp")
    swapped = [
        tuple(a.T if n == 3 else a for n, a in enumerate(group)) for group in (masters, firsts, seconds)
    ]
    table = scratch_table()
    hbm = pl.BlockSpec(memory_space=pltpu.HBM)
    ins = dict(
        cap_h=captions.reshape(rows, width_all), tok_h=token_ids.T, pair_h=pairing.reshape(1, cap_rows),
        low_h=low_images.transpose(1, 0, 2), high_h=high_images, fqkv_h=frozen_qkv, fout_h=frozen_out,
        fup_h=frozen_up, fdown_h=frozen_down, fg_h=frozen_gains,
    )
    for key, group in zip(("m", "fi", "se"), swapped):
        ins.update(zip((key + part for part in ("q_h", "o_h", "u_h", "d_h", "n_h")), group))
    results = dict(
        ig_o=jax.ShapeDtypeStruct((rows, width_all), F32),
        gsh_o=jax.ShapeDtypeStruct((3, 96, width_all), F32),
        gn_o=jax.ShapeDtypeStruct((8, 128), F32),
        tot_o=jax.ShapeDtypeStruct((8, 128), F32),
    )
    names = tuple(ins) + tuple(results) + tuple(table)
    grad_in, gsh, gn, tot = pl.pallas_call(
        partial(step_kernel, names, total_caps),
        out_shape=tuple(results.values()),
        in_specs=[hbm] * len(ins),
        out_specs=tuple([hbm] * len(results)),
        scratch_shapes=list(table.values()),
        compiler_params=pltpu.CompilerParams(
            collective_id=0, has_side_effects=True, vmem_limit_bytes=62 * 1024 * 1024
        ),
    )(*ins.values())
    operands = (gsh, gn, tot, *swapped[0], *swapped[1], *swapped[2])
    shapes = [m.shape for m in swapped[0]]
    made = [jax.ShapeDtypeStruct(shape, kind) for kind in (F32, F32, BF, F32, F32) for shape in shapes]
    made.append(jax.ShapeDtypeStruct((2, 10), F32))
    outs = pl.pallas_call(
        lamb_kernel,
        out_shape=tuple(made) + (jax.ShapeDtypeStruct(grad_in.shape, F32),),
        in_specs=[hbm] * 19,
        out_specs=tuple([hbm] * 27),
        scratch_shapes=[pltpu.VMEM(a.shape, a.dtype) for a in operands]
        + [pltpu.VMEM(m.shape, m.dtype) for m in made]
        + [
            pltpu.VMEM(grad_in.shape, F32), pltpu.SemaphoreType.DMA((22,)), pltpu.SemaphoreType.DMA((30,))
        ],
        compiler_params=pltpu.CompilerParams(vmem_limit_bytes=62 * 1024 * 1024),
    )(*operands, grad_in)
    final = [out.T if n % 5 == 3 and n < 25 else out for n, out in enumerate(outs)]
    return (final[26].reshape(captions.shape), *final[:26])


def solution(mesh):
    whole = mesh.shape["dp"] == 8 and mesh.shape["mp"] == 4
    return jax.shard_map(
        fused_shards if whole else shards,
        mesh=mesh,
        in_specs=(
            P("dp", None, None),
            P("dp", None),
            P("dp"),
            P(("dp", "mp"), None, None),
            P(("dp", "mp"), None, None),
            P(),
            P(),
            P(),
            P(),
            P(),
            P(None, "dp", "mp"),
            P("mp", "dp"),
            P("dp", "mp"),
            P("mp", "dp"),
            P(None, "dp"),
            P(None, "dp", "mp"),
            P("mp", "dp"),
            P("dp", "mp"),
            P("mp", "dp"),
            P(None, "dp"),
            P(None, "dp", "mp"),
            P("mp", "dp"),
            P("dp", "mp"),
            P("mp", "dp"),
            P(None, "dp"),
        ),
        out_specs=(
            P("dp", None, None),
            P(None, "dp", "mp"),
            P("mp", "dp"),
            P("dp", "mp"),
            P("mp", "dp"),
            P(None, "dp"),
            P(None, "dp", "mp"),
            P("mp", "dp"),
            P("dp", "mp"),
            P("mp", "dp"),
            P(None, "dp"),
            P(None, "dp", "mp"),
            P("mp", "dp"),
            P("dp", "mp"),
            P("mp", "dp"),
            P(None, "dp"),
            P(None, "dp", "mp"),
            P("mp", "dp"),
            P("dp", "mp"),
            P("mp", "dp"),
            P(None, "dp"),
            P(None, "dp", "mp"),
            P("mp", "dp"),
            P("dp", "mp"),
            P("mp", "dp"),
            P(None, "dp"),
            P(),
        ),
        check_vma=False,
    )
```

```python
from functools import partial
from types import SimpleNamespace

import jax
import jax.numpy as jnp
from jax import lax
from jax.experimental import pallas as pl
from jax.experimental.pallas import tpu as pltpu
from jax.sharding import PartitionSpec as P

HEAD_DIM = 64
STEP = 5


logit_scale = 48.0
learning_rate = 0.5
weight_decay = 0.01


def layer_norm(inputs, gain, shift):
    centre = inputs - jnp.mean(inputs, axis=-1, keepdims=True)
    spread = jnp.mean(centre * centre, axis=-1, keepdims=True)
    return centre * lax.rsqrt(spread + 1e-05) * gain + shift


def frozen_embed(rows, frozen_qkv, frozen_out, frozen_up, frozen_down, frozen_gains):
    batch_rows, seq_rows, width_all = rows.shape
    head_count = width_all // HEAD_DIM
    inputs = rows.astype(jnp.float32)
    normed = layer_norm(inputs, frozen_gains[0], 0.0).astype(jnp.bfloat16)
    projected = jnp.einsum(
        "bld,tde->tble", normed, frozen_qkv, preferred_element_type=jnp.float32
    ).astype(jnp.bfloat16)
    heads_all = projected.reshape(3, batch_rows, seq_rows, head_count, HEAD_DIM)
    scores = jnp.einsum(
        "bqhd,bkhd->bhqk", heads_all[0], heads_all[1], preferred_element_type=jnp.float32
    ) * HEAD_DIM ** (-0.5)
    weights_soft = jax.nn.softmax(scores, axis=-1).astype(jnp.bfloat16)
    context = jnp.einsum(
        "bhqk,bkhd->bqhd", weights_soft, heads_all[2], preferred_element_type=jnp.float32
    )
    context = context.reshape(batch_rows, seq_rows, width_all).astype(jnp.bfloat16)
    after_attn = inputs + jnp.einsum(
        "bld,de->ble", context, frozen_out, preferred_element_type=jnp.float32
    )
    normed_two = layer_norm(after_attn, frozen_gains[1], 0.0).astype(jnp.bfloat16)
    pre_act = jnp.einsum("bld,df->blf", normed_two, frozen_up, preferred_element_type=jnp.float32)
    hidden = jax.nn.gelu(pre_act, approximate=True).astype(jnp.bfloat16)
    outputs = after_attn + jnp.einsum(
        "blf,fd->bld", hidden, frozen_down, preferred_element_type=jnp.float32
    )
    leading = outputs[:, 0, :]
    return (leading * lax.rsqrt(jnp.sum(leading * leading, axis=1, keepdims=True) + 1e-06)).astype(
        jnp.bfloat16
    )


def lamb_parts(weight, grad, first, second, axes):
    mean_new = 0.9 * first + 0.1 * grad
    square_new = 0.999 * second + 0.001 * grad * grad
    update = (
        mean_new / (1.0 - 0.9**STEP) / (jnp.sqrt(square_new / (1.0 - 0.999**STEP)) + 1e-06)
        + weight_decay * weight
    )
    weight_sq = jnp.sum(weight * weight, axis=axes)
    update_sq = jnp.sum(update * update, axis=axes)
    return (update, mean_new, square_new, weight_sq.reshape(-1), update_sq.reshape(-1))


def shards(
    captions,
    token_ids,
    pairing,
    low_images,
    high_images,
    frozen_qkv,
    frozen_out,
    frozen_up,
    frozen_down,
    frozen_gains,
    master_qkv,
    master_out,
    master_up,
    master_down,
    master_norms,
    first_qkv,
    first_out,
    first_up,
    first_down,
    first_norms,
    second_qkv,
    second_out,
    second_up,
    second_down,
    second_norms,
):
    bf16 = jnp.bfloat16
    f32 = jnp.float32
    full_qkv, full_out, full_up, full_down, full_norms = (
        lax.all_gather(master_qkv.astype(bf16), "dp", axis=1, tiled=True),
        lax.all_gather(master_out.astype(bf16), "dp", axis=1, tiled=True),
        lax.all_gather(master_up.astype(bf16), "dp", axis=0, tiled=True),
        lax.all_gather(master_down.astype(bf16), "dp", axis=1, tiled=True),
        lax.all_gather(master_norms.astype(bf16), "dp", axis=1, tiled=True),
    )
    norm_vals = full_norms.astype(f32)
    low_embed = frozen_embed(
        low_images, frozen_qkv, frozen_out, frozen_up, frozen_down, frozen_gains
    )
    high_embed = frozen_embed(
        high_images, frozen_qkv, frozen_out, frozen_up, frozen_down, frozen_gains
    )
    local_images = jnp.concatenate([low_embed, high_embed], axis=0)
    cap_rows, seq_rows, width_all = captions.shape
    local_width = full_qkv.shape[2]
    local_heads = local_width // HEAD_DIM
    head_scale = HEAD_DIM ** (-0.5)
    inputs = captions.astype(f32)
    alive = (token_ids != 0).astype(f32)
    causal = jnp.tril(jnp.ones((seq_rows, seq_rows), dtype=jnp.bool_))
    keep_mask = causal[None, None] & (alive[:, None, None, :] > 0.5)
    normed_one = layer_norm(inputs, norm_vals[0], norm_vals[1]).astype(bf16)
    projected = jnp.einsum(
        "bld,tde->tble", normed_one, full_qkv, preferred_element_type=f32
    ).astype(bf16)
    heads_all = projected.reshape(3, cap_rows, seq_rows, local_heads, HEAD_DIM)
    query_heads, key_heads, value_heads = (heads_all[0], heads_all[1], heads_all[2])
    scores = (
        jnp.einsum("bqhd,bkhd->bhqk", query_heads, key_heads, preferred_element_type=f32)
        * head_scale
    )
    scores = jnp.where(keep_mask, scores, -1e30)
    weights_soft = jax.nn.softmax(scores, axis=-1)
    weights_low = weights_soft.astype(bf16)
    context = jnp.einsum("bhqk,bkhd->bqhd", weights_low, value_heads, preferred_element_type=f32)
    context = context.reshape(cap_rows, seq_rows, local_width).astype(bf16)
    attn_part = jnp.einsum("bld,de->ble", context, full_out, preferred_element_type=f32)
    after_attn = inputs + lax.psum(attn_part, "mp")
    normed_two = layer_norm(after_attn, norm_vals[2], norm_vals[3]).astype(bf16)
    pre_act = jnp.einsum("bld,df->blf", normed_two, full_up, preferred_element_type=f32)
    hidden = jax.nn.gelu(pre_act, approximate=True).astype(bf16)
    mlp_part = jnp.einsum("blf,fd->bld", hidden, full_down, preferred_element_type=f32)
    outputs = after_attn + lax.psum(mlp_part, "mp")
    counted = jnp.sum(alive, axis=1, keepdims=True)
    pooled = jnp.sum(outputs * alive[:, :, None], axis=1) / counted
    inverse = lax.rsqrt(jnp.sum(pooled * pooled, axis=1, keepdims=True) + 1e-06)
    unit = pooled * inverse
    text = unit.astype(bf16)
    images_all = lax.all_gather(local_images, ("dp", "mp"), axis=0, tiled=True)
    total_caps = images_all.shape[0]
    logits = logit_scale * jnp.dot(text, images_all.T, preferred_element_type=f32)
    row_top = jnp.max(logits, axis=1, keepdims=True)
    row_lse = row_top + jnp.log(jnp.sum(jnp.exp(logits - row_top), axis=1, keepdims=True))
    matched = (jnp.arange(total_caps, dtype=jnp.int32)[None, :] == pairing[:, None]).astype(f32)
    dlogits = (jnp.exp(logits - row_lse) - matched) / total_caps
    dscores = (logit_scale * dlogits).astype(bf16)
    dunit = jnp.dot(dscores, images_all, preferred_element_type=f32)
    dpooled = inverse * (dunit - unit * jnp.sum(unit * dunit, axis=1, keepdims=True))
    dout = (dpooled / counted)[:, None, :] * alive[:, :, None]
    dmlp = dout.astype(bf16)
    dhidden = jnp.einsum("bld,fd->blf", dmlp, full_down, preferred_element_type=f32)
    grad_down = jnp.einsum("blf,bld->fd", hidden, dmlp, preferred_element_type=f32)
    gelu_pull = jax.vjp(partial(jax.nn.gelu, approximate=True), pre_act)[1]
    dpre = gelu_pull(dhidden)[0].astype(bf16)
    grad_up = jnp.einsum("bld,blf->df", normed_two, dpre, preferred_element_type=f32)
    dnormed_two = lax.psum(
        jnp.einsum("blf,df->bld", dpre, full_up, preferred_element_type=f32), "mp"
    )
    ln_two_pull = jax.vjp(layer_norm, after_attn, norm_vals[2], norm_vals[3])[1]
    dafter_ln, dgain_two, dshift_two = ln_two_pull(dnormed_two)
    dafter = dout + dafter_ln
    dattn = dafter.astype(bf16)
    grad_out = jnp.einsum("bld,ble->de", context, dattn, preferred_element_type=f32)
    dcontext = jnp.einsum("ble,de->bld", dattn, full_out, preferred_element_type=f32).astype(bf16)
    dcontext = dcontext.reshape(cap_rows, seq_rows, local_heads, HEAD_DIM)
    dweights = jnp.einsum("bqhd,bkhd->bhqk", dcontext, value_heads, preferred_element_type=f32)
    dlogit_attn = weights_soft * (
        dweights - jnp.sum(weights_soft * dweights, axis=-1, keepdims=True)
    )
    dlogit_low = dlogit_attn.astype(bf16)
    dquery = (
        jnp.einsum("bhqk,bkhd->bqhd", dlogit_low, key_heads, preferred_element_type=f32)
        * head_scale
    ).astype(bf16)
    dkey = (
        jnp.einsum("bhqk,bqhd->bkhd", dlogit_low, query_heads, preferred_element_type=f32)
        * head_scale
    ).astype(bf16)
    dvalue = jnp.einsum(
        "bhqk,bqhd->bkhd", weights_low, dcontext, preferred_element_type=f32
    ).astype(bf16)
    dprojected = jnp.stack([dquery, dkey, dvalue]).reshape(3, cap_rows, seq_rows, local_width)
    grad_qkv = jnp.einsum("bld,tble->tde", normed_one, dprojected, preferred_element_type=f32)
    dnormed_one = lax.psum(
        jnp.einsum("tble,tde->bld", dprojected, full_qkv, preferred_element_type=f32), "mp"
    )
    ln_one_pull = jax.vjp(layer_norm, inputs, norm_vals[0], norm_vals[1])[1]
    dinput_ln, dgain_one, dshift_one = ln_one_pull(dnormed_one)
    input_grad = dafter + dinput_ln
    grad_norms_local = jnp.stack([dgain_one, dshift_one, dgain_two, dshift_two])
    local_grads = (grad_qkv, grad_out, grad_up, grad_down, grad_norms_local)
    masters = (master_qkv, master_out, master_up, master_down, master_norms)
    slice_dims = (1, 1, 0, 1, 1)
    summed = lax.psum(
        (local_grads[0], local_grads[1], local_grads[2], local_grads[3], local_grads[4]), "dp"
    )
    dp_index = lax.axis_index("dp")
    shard_grads = tuple(
        (
            lax.dynamic_slice_in_dim(
                summed[index],
                dp_index * masters[index].shape[slice_dims[index]],
                masters[index].shape[slice_dims[index]],
                slice_dims[index],
            )
            for index in range(5)
        )
    )
    firsts = (first_qkv, first_out, first_up, first_down, first_norms)
    seconds = (second_qkv, second_out, second_up, second_down, second_norms)
    axes_all = ((1, 2), (0, 1), (0, 1), (0, 1), (1,))
    parts = [
        lamb_parts(
            masters[index], shard_grads[index], firsts[index], seconds[index], axes_all[index]
        )
        for index in range(5)
    ]
    lead_flag = (lax.axis_index("mp") == 0).astype(f32)
    weight_squares = jnp.concatenate(
        [parts[0][3], parts[1][3], parts[2][3], parts[3][3], parts[4][3] * lead_flag]
    )
    update_squares = jnp.concatenate(
        [parts[0][4], parts[1][4], parts[2][4], parts[3][4], parts[4][4] * lead_flag]
    )
    total_squares = lax.psum(jnp.stack([weight_squares, update_squares]), ("dp", "mp"))
    matrix_norms = jnp.sqrt(total_squares)
    ratios = matrix_norms[0] / matrix_norms[1]
    ratio_pieces = (
        ratios[0:3].reshape(3, 1, 1),
        ratios[3],
        ratios[4],
        ratios[5],
        ratios[6:10].reshape(4, 1),
    )
    news = [
        masters[index] - learning_rate * ratio_pieces[index] * parts[index][0] for index in range(5)
    ]
    copies = [fresh.astype(bf16) for fresh in news]
    return (
        input_grad,
        shard_grads[0],
        shard_grads[1],
        shard_grads[2],
        shard_grads[3],
        shard_grads[4],
        news[0],
        news[1],
        news[2],
        news[3],
        news[4],
        copies[0],
        copies[1],
        copies[2],
        copies[3],
        copies[4],
        parts[0][1],
        parts[1][1],
        parts[2][1],
        parts[3][1],
        parts[4][1],
        parts[0][2],
        parts[1][2],
        parts[2][2],
        parts[3][2],
        parts[4][2],
        matrix_norms,
    )


MESH = pl.DeviceIdType.MESH
BF = jnp.bfloat16
F32 = jnp.float32


def nn(a, b):
    return lax.dot_general(a, b, (((1,), (0,)), ((), ())), preferred_element_type=F32)


def nt(a, b):
    return lax.dot_general(a, b, (((1,), (1,)), ((), ())), preferred_element_type=F32)


def tn(a, b):
    return lax.dot_general(a, b, (((0,), (0,)), ((), ())), preferred_element_type=F32)


def split(values):
    high = values.astype(BF)
    return jnp.concatenate([high, (values - high.astype(F32)).astype(BF)], axis=0)


def iota(shape, dim):
    return lax.broadcasted_iota(jnp.int32, shape, dim)


def stats(values):
    centre = values - jnp.mean(values, axis=-1, keepdims=True)
    return centre, lax.rsqrt(jnp.mean(centre * centre, axis=-1, keepdims=True) + 1e-05)


def gelu_pair(u):
    root = 0.7978845608028654
    square = u * u
    t = jnp.tanh(root * (u + 0.044715 * square * u))
    half = 0.5 * (1.0 + t)
    slope = half + 0.5 * u * (1.0 - t * t) * (root * (1.0 + 3.0 * 0.044715 * square))
    return u * half, slope


def gelu_only(u):
    root = 0.7978845608028654
    return 0.5 * u * (1.0 + jnp.tanh(root * (u + 0.044715 * u * u * u)))


def pack_attn(qkv_ref, out_ref):
    q, k, v = qkv_ref[0], qkv_ref[1], qkv_ref[2]
    out_t = out_ref[...].T
    return [
        q[:, 0:128],
        k[:, 0:128],
        v[:, 0:128],
        jnp.concatenate([q[:, 128:192], v[:, 128:192]], axis=1),
        jnp.concatenate([k[:, 128:192], out_t[:, 128:192]], axis=1),
        out_t[:, 0:128],
    ]


def lamb_update(weight, grad, first, second):
    mean_new = 0.9 * first + 0.1 * grad
    square_new = 0.999 * second + 0.001 * grad * grad
    update = (
        mean_new * (1.0 / (1.0 - 0.9**STEP))
        / (jnp.sqrt(square_new * (1.0 / (1.0 - 0.999**STEP))) + 1e-06)
        + weight_decay * weight
    )
    return update, mean_new, square_new


CHUNKS = 4


def scratch_table():
    vm = pltpu.VMEM
    dma = pltpu.SemaphoreType.DMA
    return dict(
        cap=vm((1024, 768), BF),
        tok=vm((16, 64), jnp.int32),
        pair=vm((1, 64), jnp.int32),
        alive=vm((8, 128), F32),
        pair_v=vm((64, 1), F32),
        fg_v=vm((2, 768), F32),
        qkv_v=vm((3, 96, 192), F32),
        out_v=vm((192, 96), F32),
        up_v=vm((96, 768), F32),
        down_v=vm((96, 768), F32),
        norms_v=vm((4, 96), F32),
        fin_v=vm((4, 96), F32),
        sen_v=vm((4, 96), F32),
        gsh=vm((3, 96, 768), F32),
        gn=vm((8, 128), F32),
        tot=vm((8, 128), F32),
        w=vm((3, 768, 768), BF),
        ns=vm((16, 128), F32),
        nsend=vm((16, 128), BF),
        nslot=vm((8, 16, 128), BF),
        normp=vm((16, 768), F32),
        mu=vm((1024, 1), F32),
        rs=vm((1024, 1), F32),
        causal=vm((128, 128), F32),
        n1=vm((1024, 768), BF),
        proj=vm((1024, 640), BF),
        p=vm((8, 3, 128, 128), F32),
        o=vm((1024, 256), BF),
        part=vm((1024, 768), F32),
        wo=vm((4, 768, 256), BF),
        oall=vm((4, CHUNKS, 128, 256), BF),
        cs=vm((CHUNKS, 128, 768), BF),
        cr1=vm((CHUNKS, 128, 768), BF),
        cr2=vm((CHUNKS, 128, 768), BF),
        xs=vm((CHUNKS, 128, 768), BF),
        xr1=vm((CHUNKS, 128, 768), BF),
        xr2=vm((CHUNKS, 128, 768), BF),
        a=vm((CHUNKS, 128, 768), F32),
        n2=vm((1024, 768), BF),
        gp=vm((1024, 768), F32),
        hs=vm((2, 32, 768), F32),
        hl=vm((128, 768), BF),
        asum=vm((32, 768), F32),
        cnt=vm((32, 128), F32),
        pp=vm((2, 32, 768), F32),
        pcr=vm((32, 768), F32),
        pxs=vm((32, 768), F32),
        pxr=vm((32, 768), F32),
        emb=vm((4, 2, 4, 16, 768), BF),
        dy=vm((2, 32, 768), BF),
        dpc=vm((32, 768), F32),
        dh=vm((2, 32, 768), F32),
        dz=vm((1024, 768), BF),
        rss=vm((3, 2, 7, 48, 768), BF),
        rsr=vm((3, 2, 7, 48, 768), BF),
        gns=vm((8, 768), F32),
        gnr=vm((8, 768), F32),
        gsl=vm((8, 8, 128), F32),
        gslr=vm((9, 8, 128), F32),
        sqd=vm((32, 8, 128), F32),
        loc=dma((15,)),
        first=dma((10,)),
        fin=dma((5,)),
        nsem=dma((8,)),
        ags=dma((3,)),
        agr=dma((3, 2, 7)),
        rsa=dma((3,)),
        rsb=dma((3, 2, 7)),
        wos=dma((3,)),
        wor=dma((10,)),
        oas=dma((1,)),
        oar=dma((3, CHUNKS)),
        arcs=dma((CHUNKS,)),
        arcr=dma((3, CHUNKS)),
        arxs=dma((CHUNKS,)),
        arxr=dma((3, CHUNKS)),
        shs=dma((3,)),
        shr=dma((3, CHUNKS)),
        pos=dma((3,)),
        por=dma((3,)),
        ems=dma((5,)),
        emr=dma((7,)),
        gss=dma((3,)),
        gsr=dma((9,)),
        sqs=dma((1,)),
        sqr=dma((31,)),
        outs=dma((CHUNKS,)),
    )


def step_kernel(names, total_caps, *refs):
    r = SimpleNamespace(**dict(zip(names, refs)))
    dp = lax.axis_index("dp")
    mp = lax.axis_index("mp")
    z, y = dp // 2, dp % 2
    x, c = mp // 2, mp % 2
    sib = (dp, x * 2 + (1 - c))
    xnb = (dp, (1 - x) * 2 + c)
    diag = (dp, (1 - x) * 2 + (1 - c))
    ynb = (z * 2 + (1 - y), mp)
    place_on_ring = z + y * (7 - 2 * z)

    def ring(k):
        q = (place_on_ring + k + 8) % 8
        return (q + (q // 4) * (7 - 2 * q)) * 2 + q // 4

    ways = ((ring(1), mp), (ring(-1), mp))
    zpeer = {k: (((z + k) % 4) * 2 + y, mp) for k in (1, 2, 3)}
    everyone = {k: ((dp * 4 + mp + k) % 32 // 4, (mp + k) % 4) for k in range(1, 32)}
    dpeer = {k: ((dp + k) % 8, mp) for k in range(1, 8)}

    def rcopy(src, dst, ssem, rsem, dev):
        return pltpu.make_async_remote_copy(
            src_ref=src, dst_ref=dst, send_sem=ssem, recv_sem=rsem,
            device_id=dev, device_id_type=MESH,
        )

    sends = []

    def go(make, at_end=True):
        copy = make()
        copy.start()
        if at_end:
            sends.append(make)
        return copy

    w = r.w

    def shard_rows(zz, yy):
        return pl.ds(pl.multiple_of((zz * 2 + yy) * 96, 96), 96)

    def own_rows(k):
        return pl.ds(pl.multiple_of(256 * k + 128 * c, 128), 128)

    def sib_rows(k):
        return pl.ds(pl.multiple_of(256 * k + 128 * (1 - c), 128), 128)

    firsts = [
        pltpu.make_async_copy(source, target, r.first.at[n])
        for n, (source, target) in enumerate(
            (
                (r.mq_h, r.qkv_v), (r.mo_h, r.out_v), (r.mn_h, r.norms_v), (r.mu_h, r.up_v),
                (r.md_h, r.down_v), (r.fg_h, r.fg_v), (r.tok_h, r.tok), (r.pair_h, r.pair),
                (r.fin_h, r.fin_v), (r.sen_h, r.sen_v),
            )
        )
    ]
    for copy in firsts:
        copy.start()
    cap_copy = pltpu.make_async_copy(r.cap_h, r.cap, r.loc.at[0])
    cap_copy.start()

    def piece(k, half):
        return pl.ds(pl.multiple_of(ring(k) * 96 + 48 * half, 16), 48)

    def ag_copy(kind, way, step, half, k):
        rows = w.at[kind, piece(k, half)]
        index = min(2 * step + half, 6)
        return rcopy(rows, rows, r.ags.at[kind], r.agr.at[kind, way, index], ways[way])

    def ag_own(kind, way):
        for half in (0, 1):
            go(partial(ag_copy, kind, way, 0, half, 0), False)

    def ag_step(kind, step, half):
        for way in (0, 1):
            if step == 3 and way != half:
                continue
            k = -step if way == 0 else step
            ag_copy(kind, way, step - 1, half, k).wait_recv()
            go(partial(ag_copy, kind, way, step, half, k), False)

    def ag_done(kind):
        ag_copy(kind, 0, 2, 1, -3).wait_recv()
        ag_copy(kind, 1, 2, 0, 3).wait_recv()
        ag_copy(kind, 0, 3, 0, -4).wait_recv()
        ag_copy(kind, 1, 3, 1, 4).wait_recv()

    def wo_x(k, source):
        rows = pl.ds(pl.multiple_of(ring(k) * 96, 16), 96)
        return rcopy(
            w.at[0, rows, pl.ds(512, 256)], r.wo.at[source(), rows], r.wos.at[0], r.wor.at[k + 3], xnb
        )

    def wo_send(*which):
        for k in which:
            go(partial(wo_x, k, lambda: mp), False)

    def wo_own(source):
        return rcopy(w.at[0, :, pl.ds(512, 256)], r.wo.at[source()], r.wos.at[1], r.wor.at[8], sib)

    def wo_across(source):
        ref = r.wo.at[source()]
        return rcopy(ref, ref, r.wos.at[2], r.wor.at[9], sib)

    def wo_cores():
        for k in range(-3, 5):
            wo_x(k, lambda: (1 - x) * 2 + c).wait_recv()
        go(lambda: wo_across(lambda: (1 - x) * 2 + c))

    def wo_done():
        wo_own(lambda: x * 2 + 1 - c).wait_recv()
        wo_across(lambda: (1 - x) * 2 + 1 - c).wait_recv()

    def o_copy(n, k, source):
        dev = (sib, xnb, diag)[n]
        rows = own_rows(k) if n == 1 else sib_rows(k)
        return rcopy(r.o.at[rows], r.oall.at[source(), k], r.oas.at[0], r.oar.at[n, k], dev)

    def o_send(k):
        for n in range(3):
            go(partial(o_copy, n, k, lambda: mp), False)
        r.oall[mp, k] = r.o[own_rows(k), :]

    def o_wait(k):
        others = (x * 2 + 1 - c, (1 - x) * 2 + c, (1 - x) * 2 + 1 - c)
        for n in range(3):
            o_copy(n, k, lambda: others[n]).wait_recv()

    def core_copy(which, k, received):
        return rcopy(r.cs.at[k], received.at[k], r.arcs.at[k], r.arcr.at[which, k], sib)

    def x_copy(which, k, received_x):
        return rcopy(r.xs.at[k], received_x.at[k], r.arxs.at[k], r.arxr.at[which, k], xnb)

    def ar_start(which, k, received):
        if which > 1:
            core_copy(which - 1, k, received).wait_send()
        r.cs[k] = r.part[sib_rows(k), :].astype(BF)
        go(lambda: core_copy(which, k, received), which == 2)

    def ar_mid(which, k, received, received_x):
        core_copy(which, k, received).wait_recv()
        if which > 1:
            x_copy(which - 1, k, received_x).wait_send()
        r.xs[k] = (r.part[own_rows(k), :] + received[k].astype(F32)).astype(BF)
        go(lambda: x_copy(which, k, received_x), which == 2)

    def ar_end(which, k, received_x):
        x_copy(which, k, received_x).wait_recv()
        return r.xs[k].astype(F32) + received_x[k].astype(F32)

    def share_copy(which, k, ref, rows):
        part = ref.at[rows(k)]
        return rcopy(part, part, r.shs.at[which], r.shr.at[which, k], sib)

    def share(which, k, ref):
        go(lambda: share_copy(which, k, ref, own_rows), False)

    def share_wait(which, k, ref):
        share_copy(which, k, ref, sib_rows).wait_recv()

    barrier = pltpu.get_barrier_semaphore()
    partners = list(everyone.values())
    for dev in partners:
        pl.semaphore_signal(barrier, inc=1, device_id=dev, device_id_type=MESH)
    for copy in firsts[0:3]:
        copy.wait()
    tiles = pack_attn(r.qkv_v, r.out_v)
    mine = shard_rows(z, y)
    for t in range(6):
        w[0, mine, 128 * t : 128 * (t + 1)] = tiles[t].astype(BF)
    r.ns[...] = jnp.zeros((16, 128), F32)
    r.ns[0:4, 0:96] = r.norms_v[...]
    r.nsend[...] = r.ns[...].astype(BF)
    r.nslot[dp] = r.nsend[...]

    pl.semaphore_wait(barrier, len(partners))

    def norm_copy(k, source):
        return rcopy(
            r.nsend, r.nslot.at[source()], r.nsem.at[7], r.nsem.at[k - 1], dpeer[k]
        )

    for k in range(1, 8):
        go(partial(norm_copy, k, lambda: dp), False)
    for way in (0, 1):
        ag_own(0, way)
    for copy in firsts[3:10]:
        copy.wait()
    w[1, mine, :] = r.up_v[...].astype(BF)
    w[2, mine, :] = r.down_v[...].astype(BF)

    live = jnp.where(r.tok[...] != 0, 1.0, 0.0).astype(BF)
    spread_caps = jnp.where(iota((64, 1024), 1) // 16 == iota((64, 1024), 0), 1.0, 0.0).astype(BF)
    live_all = nn(live, spread_caps)
    live_row = jnp.sum(
        jnp.where(iota((16, 1024), 1) % 16 == iota((16, 1024), 0), live_all, 0.0), axis=0, keepdims=True
    )
    for b in range(8):
        r.alive[b : b + 1, :] = live_row[:, 128 * b : 128 * (b + 1)]
    image = r.pair[...]
    owner_dp = image // 64
    column = ((((image // 16) % 4) * 2 + owner_dp % 2) * 4 + owner_dp // 2) * 16 + image % 16
    order = iota((64, 64), 0)
    caption = 16 * ((order % 32) // 8) + 8 * (order // 32) + order % 8
    r.pair_v[...] = jnp.sum(
        jnp.where(iota((64, 64), 1) == caption, column.astype(F32), 0.0), axis=1, keepdims=True
    )

    rows_i = iota((128, 128), 0)
    lanes_i = iota((128, 128), 1)
    r.causal[...] = jnp.where(
        (rows_i // 16 == lanes_i // 16) & (lanes_i <= rows_i), 1.0, 0.0
    ).astype(F32)

    def emb_copy(index, dev, pick):
        ref = pick()
        return rcopy(ref, ref, r.ems.at[max(index - 2, 0)], r.emr.at[index], dev)

    def image_phase(iq, io, iu, idn, low, high, qt, pn, x0, lows):
        copies = [
            pltpu.make_async_copy(r.fqkv_h, iq, r.loc.at[1]),
            pltpu.make_async_copy(r.high_h, high, r.loc.at[2]),
            pltpu.make_async_copy(r.low_h, low, r.loc.at[3]),
            pltpu.make_async_copy(r.fout_h, io, r.loc.at[4]),
            pltpu.make_async_copy(r.fup_h, iu, r.loc.at[5]),
            pltpu.make_async_copy(r.fdown_h, idn, r.loc.at[6]),
        ]
        for copy in copies:
            copy.start()
        copies[1].wait()
        copies[2].wait()
        g1 = r.fg_v[0:1, :]
        g2 = r.fg_v[1:2, :]
        x0[0:2, :] = low[0].astype(F32)
        for n in range(50):
            lows[2 * n : 2 * n + 2, :] = low[n].astype(F32)
        for b in range(14):
            x0[b + 2 : b + 3, :] = high[b, 0:1, :].astype(F32)
        centre, inv = stats(x0[...])
        first = (centre * inv * g1).astype(BF)
        copies[0].wait()
        query = nn(first, iq[0]).astype(BF).astype(F32) * 0.125
        head = iota((16, 768), 1) // 64 == iota((16, 768), 0)
        spread = jnp.concatenate(
            [jnp.where(head, query[b : b + 1, :], 0.0).astype(BF) for b in range(16)], axis=0
        )
        qt[...] = nt(spread, iq[1]).astype(BF)

        def attend(rows, slot, keep=None):
            centre, inv = stats(rows)
            normed = (centre * inv * g1).astype(BF)
            at = pl.ds(pl.multiple_of(slot * 16, 16), 16)
            scores = nt(qt[at, :], normed)
            if keep is not None:
                scores = jnp.where(keep, scores, -1e30)
            e = jnp.exp(scores - jnp.max(scores, axis=-1, keepdims=True))
            soft = (e / jnp.sum(e, axis=-1, keepdims=True)).astype(BF)
            pn[at, :] = nn(soft, normed).astype(BF)

        for b in range(2):
            attend(lows[...], b, iota((16, 100), 1) % 2 == b)

        def some(b, carry):
            attend(high[b].astype(F32), b + 2)
            return carry

        wo_send(0)
        ag_step(0, 1, 0)
        lax.fori_loop(0, 2, some, 0)
        ag_step(0, 1, 1)
        wo_send(1, -1)
        lax.fori_loop(2, 5, some, 0)
        ag_step(0, 2, 0)
        lax.fori_loop(5, 7, some, 0)
        ag_step(0, 2, 1)
        wo_send(2, -2)
        lax.fori_loop(7, 10, some, 0)
        ag_step(0, 3, 0)
        ag_own(1, 0)
        text_norm()
        ag_step(0, 3, 1)
        ag_own(1, 1)
        lax.fori_loop(10, 14, some, 0)
        ag_done(0)
        wo_send(3, -3, 4)
        go(lambda: wo_own(lambda: mp))
        r.wo[mp] = w[0, :, 512:768]
        attention_forward(0)
        ag_step(1, 1, 0)
        attention_forward(1)
        values = nn(pn[...], iq[2])
        head_all = iota((256, 768), 1) // 64 == iota((256, 768), 0) % 16
        picked = jnp.where(head_all, values, 0.0).astype(BF)
        chooser = jnp.where(iota((16, 256), 1) // 16 == iota((16, 256), 0), 1.0, 0.0).astype(BF)
        context = nn(chooser, picked).astype(BF)
        copies[3].wait()
        after = x0[...] + nn(context, io[...])
        centre, inv = stats(after)
        second = (centre * inv * g2).astype(BF)
        ag_step(1, 1, 1)
        copies[4].wait()
        copies[5].wait()
        leading = after
        for t in range(4):
            cols = slice(768 * t, 768 * (t + 1))
            hidden = gelu_only(nn(second, iu[:, cols])).astype(BF)
            leading = leading + nn(hidden, idn[cols, :])
        norm = lax.rsqrt(jnp.sum(leading * leading, axis=1, keepdims=True) + 1e-06)
        r.emb[mp, y, z] = (leading * norm).astype(BF)
        for k in (1, 2, 3):
            go(partial(emb_copy, k - 1, zpeer[k], lambda: r.emb.at[mp, y, z]), False)
        attention_forward(2)
        ag_step(1, 2, 0)
        attention_forward(3)
        ag_step(1, 2, 1)
        ag_step(1, 3, 0)
        ag_own(2, 0)

    def emb_y():
        for k in (1, 2, 3):
            emb_copy(k - 1, zpeer[k], lambda: r.emb.at[mp, y, (z - k + 4) % 4]).wait_recv()
        go(lambda: emb_copy(3, ynb, lambda: r.emb.at[mp, y]))

    def emb_x():
        emb_copy(3, ynb, lambda: r.emb.at[mp, 1 - y]).wait_recv()
        go(lambda: emb_copy(4, xnb, lambda: r.emb.at[mp]))
        go(lambda: emb_copy(5, sib, lambda: r.emb.at[mp]))

    def emb_c():
        emb_copy(4, xnb, lambda: r.emb.at[(1 - x) * 2 + c]).wait_recv()
        go(lambda: emb_copy(6, sib, lambda: r.emb.at[(1 - x) * 2 + c]))

    def emb_done():
        emb_copy(5, sib, lambda: r.emb.at[x * 2 + 1 - c]).wait_recv()
        emb_copy(6, sib, lambda: r.emb.at[(1 - x) * 2 + 1 - c]).wait_recv()

    def text_norm():
        for k in range(1, 8):
            norm_copy(k, lambda: (dp - k + 8) % 8).wait_recv()
        place_r = iota((1024, 768), 0)
        place = jnp.where(
            (iota((1024, 768), 1) == (place_r // 128) * 96 + place_r % 128) & (place_r % 128 < 96), 1.0, 0.0
        ).astype(BF)
        r.normp[...] = nn(jnp.concatenate([r.nslot[i] for i in range(8)], axis=1), place)
        cap_copy.wait()
        for k in range(CHUNKS):
            rows = slice(256 * k, 256 * (k + 1))
            values = r.cap[rows, :].astype(F32)
            mu = jnp.mean(values, axis=-1, keepdims=True)
            centre = values - mu
            inv = lax.rsqrt(jnp.mean(centre * centre, axis=-1, keepdims=True) + 1e-05)
            r.mu[rows, :] = mu
            r.rs[rows, :] = inv
            r.n1[rows, :] = (centre * inv * r.normp[0:1, :] + r.normp[1:2, :]).astype(BF)

    lane = iota((1, 128), 1)
    lo = jnp.where(lane < 64, 1.0, 0.0).astype(BF)
    hi = jnp.where(lane < 64, 0.0, 1.0).astype(BF)
    is_lo = iota((128, 128), 1) < 64

    def attention_forward(k):
        rows = slice(256 * k, 256 * (k + 1))
        r.proj[rows, :] = nn(r.n1[rows, :], w[0, :, 0:640]).astype(BF)
        for b in (2 * k, 2 * k + 1):
            at = slice(128 * b, 128 * (b + 1))
            t = [r.proj[at, 128 * i : 128 * (i + 1)] for i in range(5)]
            keep = (r.causal[...] * r.alive[b : b + 1, :]) > 0.5
            probs = []
            for h, (left, right) in enumerate(((t[0] * lo, t[1]), (t[0] * hi, t[1]), (t[3] * lo, t[4]))):
                s = jnp.where(keep, nt(left, right) * 0.125, -1e30)
                e = jnp.exp(s - jnp.max(s, axis=-1, keepdims=True))
                p = e * (1.0 / jnp.sum(e, axis=-1, keepdims=True))
                r.p[b, h] = p
                probs.append(p.astype(BF))
            pair = nn(
                jnp.concatenate([probs[0], probs[1]], axis=1),
                jnp.concatenate([t[2] * lo, t[2] * hi], axis=0),
            )
            r.o[at, 0:128] = nn(probs[2], t[3] * hi).astype(BF)
            r.o[at, 128:256] = pair.astype(BF)
        o_send(k)

    def own_alive(k):
        row = r.alive[pl.ds(2 * k + c, 1), :]
        return jnp.where(iota((8, 128), 1) // 16 == iota((8, 128), 0), row, 0.0)

    def chunk_alive(k):
        row = jnp.concatenate([r.alive[2 * k : 2 * k + 1, :], r.alive[2 * k + 1 : 2 * k + 2, :]], axis=1)
        return jnp.where(iota((16, 256), 1) // 16 == iota((16, 256), 0), row, 0.0).astype(BF)

    def second_norm(k):
        o_wait(k)
        terms = [nt(r.oall[j, k], r.wo[j]) for j in range(4)]
        a = r.cap[own_rows(k), :].astype(F32) + ((terms[0] + terms[1]) + (terms[2] + terms[3]))
        r.a[k] = a
        centre, inv = stats(a)
        r.n2[own_rows(k), :] = (centre * inv * r.normp[2:3, :] + r.normp[3:4, :]).astype(BF)
        share(0, k, r.n2)
        alive = own_alive(k)
        at = slice(8 * k, 8 * (k + 1))
        r.asum[at, :] = nn(jnp.concatenate([alive, alive], axis=1).astype(BF), split(a))
        r.cnt[at, :] = jnp.broadcast_to(jnp.sum(alive, axis=1, keepdims=True), (8, 128))

    def mlp_up(k):
        rows = slice(256 * k, 256 * (k + 1))
        share_wait(0, k, r.n2)
        value, slope = gelu_pair(nn(r.n2[rows, :], w[1]))
        r.gp[rows, :] = slope
        sums = nn(chunk_alive(k), value.astype(BF))
        r.hs[0, 8 * k : 8 * (k + 1), :] = sums[0:8]
        r.hs[1, 8 * k : 8 * (k + 1), :] = sums[8:16]

    pl.run_scoped(
        image_phase,
        pltpu.VMEM((3, 768, 768), BF),
        pltpu.VMEM((768, 768), BF),
        pltpu.VMEM((768, 3072), BF),
        pltpu.VMEM((3072, 768), BF),
        pltpu.VMEM((50, 2, 768), BF),
        pltpu.VMEM((14, 145, 768), BF),
        pltpu.VMEM((256, 768), BF),
        pltpu.VMEM((256, 768), BF),
        pltpu.VMEM((16, 768), F32),
        pltpu.VMEM((100, 768), F32),
    )

    ag_step(1, 3, 1)
    ag_own(2, 1)
    wo_cores()
    wo_done()
    second_norm(0)
    ag_done(1)
    ag_step(2, 1, 0)
    mlp_up(0)
    second_norm(1)
    ag_step(2, 1, 1)
    emb_y()
    mlp_up(1)
    ag_step(2, 2, 0)
    second_norm(2)
    ag_step(2, 2, 1)
    emb_x()
    mlp_up(2)
    ag_step(2, 3, 0)
    second_norm(3)
    ag_step(2, 3, 1)
    emb_c()
    mlp_up(3)

    hsum = r.hs[...].reshape(64, 768)
    high_part = hsum.astype(BF)
    r.hl[0:64, :] = high_part
    r.hl[64:128, :] = (hsum - high_part.astype(F32)).astype(BF)
    ag_done(2)
    both = nt(r.hl[...], w[2])
    r.pp[...] = (both[0:64] + both[64:128]).reshape(2, 32, 768)
    first_copy = go(lambda: rcopy(r.pp.at[1 - c], r.pcr, r.pos.at[0], r.por.at[0], sib))
    emb_done()
    first_copy.wait_recv()
    r.pxs[...] = r.pp[c] + r.pcr[...]
    second_copy = go(lambda: rcopy(r.pxs, r.pxr, r.pos.at[1], r.por.at[1], xnb))
    count = r.cnt[:, 0:1]
    second_copy.wait_recv()
    pooled = (r.asum[...] + (r.pxs[...] + r.pxr[...])) / count
    inverse = lax.rsqrt(jnp.sum(pooled * pooled, axis=1, keepdims=True) + 1e-06)
    unit = pooled * inverse
    images = r.emb[...].reshape(total_caps, 768)
    logits = logit_scale * nt(unit.astype(BF), images)
    top = jnp.max(logits, axis=1, keepdims=True)
    row_lse = top + jnp.log(jnp.sum(jnp.exp(logits - top), axis=1, keepdims=True))
    match = iota((32, total_caps), 1).astype(F32) == r.pair_v[pl.ds(pl.multiple_of(32 * c, 32), 32), :]
    dlogits = (jnp.exp(logits - row_lse) - jnp.where(match, 1.0, 0.0)) / total_caps
    dunit = nn((logit_scale * dlogits).astype(BF), images)
    dpooled = inverse * (dunit - unit * jnp.sum(unit * dunit, axis=1, keepdims=True))
    dpc = dpooled / count
    r.dpc[...] = dpc
    r.dy[c] = dpc.astype(BF)

    def dy_copy(core):
        ref = r.dy.at[core]
        return rcopy(ref, ref, r.pos.at[2], r.por.at[2], sib)

    go(lambda: dy_copy(c))

    def backward(du, dpack, g, packed, raw):
        moments = ((r.fiq_h, r.fio_h, r.fiu_h, r.fid_h), (r.seq_h, r.seo_h, r.seu_h, r.sed_h))
        raw_copies = []
        for m in range(2):
            for n in range(4):
                copy = pltpu.make_async_copy(moments[m][n], raw[4 * m + n], r.loc.at[7 + 4 * m + n])
                copy.start()
                raw_copies.append(copy)

        def mlp_backward(k):
            rows = slice(256 * k, 256 * (k + 1))
            dh = jnp.concatenate(
                [r.dh[0, 8 * k : 8 * (k + 1), :], r.dh[1, 8 * k : 8 * (k + 1), :]], axis=0
            )
            dh_high = dh.astype(BF)
            dh_low = (dh - dh_high.astype(F32)).astype(BF)
            alive = chunk_alive(k)
            spread = tn(jnp.concatenate([alive, alive], axis=0), jnp.concatenate([dh_high, dh_low], axis=0))
            value = (r.gp[rows, :] * spread).astype(BF)
            du[rows, :] = value
            r.part[rows, :] = nt(value, w[1])
            ar_start(1, k, r.cr2)

        def rs_copy(kind, way, index):
            return rcopy(
                r.rss.at[kind, way, index], r.rsr.at[kind, way, index],
                r.rsa.at[kind], r.rsb.at[kind, way, index], ways[way],
            )

        def rs_index(step, half):
            return 0 if step == 0 else 2 * step - 1 + half

        def rs_send(kind, way, step, half, add):
            k = 4 - step if way == 0 else step - 4
            value = g[kind, piece(k, half), :]
            if add:
                before = rs_index(step - 1, half)
                rs_copy(kind, way, before).wait_recv()
                value = value + r.rsr[kind, way, before].astype(F32)
            index = rs_index(step, half)
            r.rss[kind, way, index] = value.astype(BF)
            go(partial(rs_copy, kind, way, index), False)

        def rs_start(kind):
            for way in (0, 1):
                rs_send(kind, way, 0, way, False)
            for way in (0, 1):
                rs_send(kind, way, 1, 1 - way, False)

        def rs_step(kind, step, early):
            for way in (0, 1):
                rs_send(kind, way, step, 1 - way if early else way, True)

        def rs_end(kind):
            for half in (0, 1):
                index = rs_index(3, half)
                for way in (0, 1):
                    rs_copy(kind, way, index).wait_recv()
                r.gsh[kind, 48 * half : 48 * half + 48, :] = g[kind, piece(0, half), :] + (
                    r.rsr[kind, 0, index].astype(F32) + r.rsr[kind, 1, index].astype(F32)
                )

        def second_backward(k, dgain, dshift):
            dn = ar_end(1, k, r.xr2)
            centre, inv = stats(r.a[k])
            hat = centre * inv
            dhat = dn * r.normp[2:3, :]
            dln = inv * (
                dhat - jnp.mean(dhat, axis=-1, keepdims=True)
                - hat * jnp.mean(dhat * hat, axis=-1, keepdims=True)
            )
            alive = own_alive(k)
            dout = tn(
                jnp.concatenate([alive, alive], axis=0).astype(BF), split(r.dpc[8 * k : 8 * (k + 1), :])
            )
            da = dout + dln
            r.a[k] = da
            r.dz[own_rows(k), :] = da.astype(BF)
            share(1, k, r.dz)
            return (
                dgain + jnp.sum(dn * hat, axis=0, keepdims=True),
                dshift + jnp.sum(dn, axis=0, keepdims=True),
            )

        def attention_backward(k, dgain, dshift):
            rows = slice(256 * k, 256 * (k + 1))
            share_wait(1, k, r.dz)
            do_all = nn(r.dz[rows, :], w[0, :, 512:768]).astype(BF)
            for i, b in enumerate((2 * k, 2 * k + 1)):
                at = slice(128 * b, 128 * (b + 1))
                t = [r.proj[at, 128 * j : 128 * (j + 1)] for j in range(5)]
                do2 = do_all[128 * i : 128 * (i + 1), 0:128] * hi
                do01 = do_all[128 * i : 128 * (i + 1), 128:256]
                ds, ps = [], []
                for h, (left, right) in enumerate(((do01 * lo, t[2]), (do01 * hi, t[2]), (do2, t[3]))):
                    dw = nt(left, right)
                    p = r.p[b, h]
                    ps.append(p.astype(BF))
                    ds.append((p * (dw - jnp.sum(p * dw, axis=-1, keepdims=True))).astype(BF))
                dq = nn(
                    jnp.concatenate([ds[0], ds[1]], axis=1),
                    jnp.concatenate([t[1] * lo, t[1] * hi], axis=0),
                )
                dk = tn(
                    jnp.concatenate([ds[0], ds[1]], axis=0),
                    jnp.concatenate([t[0] * lo, t[0] * hi], axis=0),
                )
                dv = tn(
                    jnp.concatenate([ps[0], ps[1]], axis=0),
                    jnp.concatenate([do01 * lo, do01 * hi], axis=0),
                )
                dq2 = nn(ds[2], t[4] * lo)
                dk2 = tn(ds[2], t[3] * lo)
                dv2 = tn(ps[2], do2)
                dpack[at, 0:128] = (dq * 0.125).astype(BF)
                dpack[at, 128:256] = (dk * 0.125).astype(BF)
                dpack[at, 256:384] = dv.astype(BF)
                dpack[at, 384:512] = (dq2 * 0.125 + dv2).astype(BF)
                dpack[at, 512:640] = (dk2 * 0.125).astype(BF)
            part = nt(dpack[rows, :], w[0, :, 0:640])
            r.part[rows, :] = part
            ar_start(2, k, r.cr1)
            inner = tn(r.n1[rows, :], dpack[rows, :])
            outer = tn(r.dz[rows, :], r.o[rows, :])
            if k == 0:
                g[0, :, 0:512] = inner[:, 0:512]
                g[0, :, 512:640] = inner[:, 512:640] + outer[:, 0:128]
                g[0, :, 640:768] = outer[:, 128:256]
            else:
                g[0, :, 0:512] += inner[:, 0:512]
                g[0, :, 512:640] += inner[:, 512:640] + outer[:, 0:128]
                g[0, :, 640:768] += outer[:, 128:256]
            hat = (r.cap[rows, :].astype(F32) - r.mu[rows, :]) * r.rs[rows, :]
            return (
                dgain + jnp.sum(part * hat, axis=0, keepdims=True),
                dshift + jnp.sum(part, axis=0, keepdims=True),
            )

        dy_copy(1 - c).wait_recv()
        dy = r.dy[...].reshape(64, 768)
        g[2] = tn(jnp.concatenate([dy, dy], axis=0), r.hl[...])
        rs_start(2)
        r.dh[...] = nn(dy, w[2]).reshape(2, 32, 768)

        mlp_backward(0)
        ar_mid(1, 0, r.cr2, r.xr2)
        mlp_backward(1)
        rs_step(2, 1, False)
        ar_mid(1, 1, r.cr2, r.xr2)
        mlp_backward(2)
        rs_step(2, 2, True)
        mlp_backward(3)
        ar_mid(1, 2, r.cr2, r.xr2)
        rs_step(2, 2, False)
        ar_mid(1, 3, r.cr2, r.xr2)
        g[1] = tn(r.n2[...], du[...])
        rs_start(1)
        rs_step(2, 3, True)
        zero = jnp.zeros((1, 768), F32)
        dg2, db2, dg1, db1 = zero, zero, zero, zero
        dg2, db2 = second_backward(0, dg2, db2)
        rs_step(2, 3, False)
        dg1, db1 = attention_backward(0, dg1, db1)
        dg2, db2 = second_backward(1, dg2, db2)
        ar_mid(2, 0, r.cr1, r.xr1)
        rs_step(1, 1, False)
        rs_end(2)
        dg1, db1 = attention_backward(1, dg1, db1)
        rs_step(1, 2, True)
        dg2, db2 = second_backward(2, dg2, db2)
        ar_mid(2, 1, r.cr1, r.xr1)
        rs_step(1, 2, False)
        dg1, db1 = attention_backward(2, dg1, db1)
        rs_step(1, 3, True)
        dg2, db2 = second_backward(3, dg2, db2)
        ar_mid(2, 2, r.cr1, r.xr1)
        rs_step(1, 3, False)
        dg1, db1 = attention_backward(3, dg1, db1)
        rs_start(0)
        ar_mid(2, 3, r.cr1, r.xr1)

        def gn_core():
            return rcopy(r.gns, r.gnr, r.gss.at[0], r.gsr.at[7], sib)

        def gn_slice(k):
            return rcopy(r.gsl.at[(dp + k) % 8], r.gslr.at[k - 1], r.gss.at[1], r.gsr.at[k - 1], dpeer[k])

        def gn_x():
            return rcopy(r.gslr.at[7], r.gslr.at[8], r.gss.at[2], r.gsr.at[8], xnb)

        r.gns[...] = jnp.concatenate(
            [dg1, db1, 0.5 * dg2, 0.5 * db2, jnp.zeros((4, 768), F32)], axis=0
        )
        go(gn_core)

        def out_copy(k, rows):
            return rcopy(
                r.a.at[k], r.ig_o.at[rows(k)], r.shs.at[2], r.shr.at[2, k], sib
            )

        def finish_rows(k):
            dn = ar_end(2, k, r.xr1)
            hat = (r.cap[own_rows(k), :].astype(F32) - r.mu[own_rows(k), :]) * r.rs[own_rows(k), :]
            dhat = dn * r.normp[0:1, :]
            dln = r.rs[own_rows(k), :] * (
                dhat - jnp.mean(dhat, axis=-1, keepdims=True)
                - hat * jnp.mean(dhat * hat, axis=-1, keepdims=True)
            )
            r.a[k] = r.a[k] + dln
            local = pltpu.make_async_copy(r.a.at[k], r.ig_o.at[own_rows(k)], r.outs.at[k])
            local.start()
            go(lambda: out_copy(k, own_rows), False)
            return local

        for t, tile in enumerate(tiles):
            packed[0, 0, :, 128 * t : 128 * (t + 1)] = tile
        packed[0, 1] = r.up_v[...]
        packed[0, 2] = r.down_v[...]
        for copy in raw_copies:
            copy.wait()
        for m in range(2):
            for t, tile in enumerate(pack_attn(raw[4 * m], raw[4 * m + 1])):
                packed[1 + m, 0, :, 128 * t : 128 * (t + 1)] = tile
            packed[1 + m, 1] = raw[4 * m + 2][...]
            packed[1 + m, 2] = raw[4 * m + 3][...]

        gn_core().wait_recv()
        gn_pad = jnp.concatenate([r.gns[...] + r.gnr[...], jnp.zeros((8, 128), F32)], axis=1)
        for i in range(8):
            r.gsl[i] = gn_pad[:, 96 * i : 96 * i + 128]
        for k in range(1, 8):
            go(partial(gn_slice, k), False)
        rs_step(0, 1, False)
        locals_out = [finish_rows(0)]
        rs_step(0, 2, True)
        locals_out.append(finish_rows(1))
        rs_end(1)
        rs_step(0, 2, False)
        gn_mine = r.gsl[dp]
        for k in range(1, 8):
            gn_slice(k).wait_recv()
            gn_mine = gn_mine + r.gslr[k - 1]
        r.gslr[7] = gn_mine
        go(gn_x)
        locals_out.append(finish_rows(2))
        rs_step(0, 3, True)
        locals_out.append(finish_rows(3))
        rs_step(0, 3, False)
        gn_x().wait_recv()
        gn_mine = jnp.where(iota((8, 128), 1) < 96, gn_mine + r.gslr[8], 0.0)
        r.gn[...] = gn_mine
        finals = [pltpu.make_async_copy(r.gn, r.gn_o, r.fin.at[3])]
        finals[0].start()

        sel_lane = iota((8, 128), 1)
        sel_row = iota((8, 128), 0)
        squares = jnp.zeros((8, 128), F32)

        def put(acc, row, index, value):
            return acc + jnp.where((sel_row == row) & (sel_lane == index), value, 0.0)

        quarter = 0.25
        zeros4 = jnp.zeros((4, 96), F32)
        gn4 = gn_mine[0:4, 0:96]
        norm_update, _, _ = lamb_update(r.norms_v[...], gn4, r.fin_v[...], r.sen_v[...])
        for row, value in ((0, r.norms_v[...]), (1, norm_update)):
            line = quarter * jnp.sum(value * value, axis=1, keepdims=True)
            for n in range(4):
                squares = put(squares, row, 6 + n, line[n : n + 1, :])
        lane_all = iota((1, 768), 1)
        third = (lane_all // 64) % 12
        owner = jnp.where(
            lane_all < 384, lane_all // 128,
            jnp.where(
                lane_all < 512, jnp.where(lane_all < 448, 0, 2),
                jnp.where(lane_all < 576, 1, 3),
            ),
        )
        for kind in (2, 1, 0):
            if kind == 0:
                rs_end(0)
            final = pltpu.make_async_copy(r.gsh.at[kind], r.gsh_o.at[kind], r.fin.at[kind])
            final.start()
            finals.append(final)
            update, _, _ = lamb_update(packed[0, kind], r.gsh[kind], packed[1, kind], packed[2, kind])
            for row, value in ((0, packed[0, kind]), (1, update)):
                line = jnp.sum(value * value, axis=0, keepdims=True)
                if kind == 0:
                    for n in range(4):
                        part = jnp.sum(jnp.where(owner == n, line, 0.0), axis=1, keepdims=True)
                        squares = put(squares, row, n, part)
                else:
                    squares = put(squares, row, 3 + kind, jnp.sum(line, axis=1, keepdims=True))

        def sq_copy(k, slot):
            ref = r.sqd.at[slot]
            return rcopy(ref, ref, r.sqs.at[0], r.sqr.at[k - 1], everyone[k])

        me = dp * 4 + mp
        r.sqd[me] = squares
        for k in range(1, 32):
            go(partial(sq_copy, k, me), False)
        for k in range(1, 32):
            sq_copy(k, (me - k + 32) % 32).wait_recv()
        r.tot[...] = jnp.sum(r.sqd[...], axis=0)
        final = pltpu.make_async_copy(r.tot, r.tot_o, r.fin.at[4])
        final.start()
        finals.append(final)
        for local in locals_out + finals:
            local.wait()
        for k in range(CHUNKS):
            out_copy(k, sib_rows).wait_recv()

    pl.run_scoped(
        backward,
        pltpu.VMEM((1024, 768), BF),
        pltpu.VMEM((1024, 640), BF),
        pltpu.VMEM((3, 768, 768), F32),
        pltpu.VMEM((3, 3, 96, 768), F32),
        [
            pltpu.VMEM(shape, F32)
            for _ in range(2)
            for shape in ((3, 96, 192), (192, 96), (96, 768), (96, 768))
        ],
    )
    for make in sends:
        make().wait_send()

    def all_sent(ref, sem):
        rcopy(ref, ref, sem, sem, sib).wait_send()

    all_sent(r.nslot.at[pl.ds(0, 7)], r.nsem.at[7])
    for kind in range(3):
        all_sent(w.at[kind, pl.ds(0, 672)], r.ags.at[kind])
        all_sent(r.rss.at[kind], r.rsa.at[kind])
    all_sent(r.n2.at[pl.ds(0, 512)], r.shs.at[0])
    all_sent(r.wo.at[0], r.wos.at[0])
    all_sent(r.oall.at[pl.ds(0, 3)], r.oas.at[0])
    all_sent(r.dz.at[pl.ds(0, 512)], r.shs.at[1])
    all_sent(r.a, r.shs.at[2])
    all_sent(r.emb.at[0, 0, pl.ds(0, 3)], r.ems.at[0])
    all_sent(r.gslr.at[pl.ds(0, 7)], r.gss.at[1])
    all_sent(r.sqd.at[pl.ds(0, 31)], r.sqs.at[0])


def lamb_kernel(*refs):
    sources, targets = refs[0:19], refs[19:46]
    buffers, results = refs[46:64], refs[64:90]
    rows, in_sem, out_sem = refs[90:93]
    pieces = []
    for n in range(4):
        at = pl.ds(256 * n, 256)
        pieces.append(
            (
                pltpu.make_async_copy(sources[18].at[at], rows.at[at], in_sem.at[18 + n]),
                pltpu.make_async_copy(rows.at[at], targets[26].at[at], out_sem.at[26 + n]),
            )
        )
    loads = [pltpu.make_async_copy(sources[n], buffers[n], in_sem.at[n]) for n in range(18)]
    for copy in loads:
        copy.start()
    for load, _ in pieces:
        load.start()
    stores = []
    (gsh, gn, tot, w_qkv, w_out, w_up, w_down, w_norms, m_qkv, m_out, m_up, m_down, m_norms,
     v_qkv, v_out, v_up, v_down, v_norms) = buffers
    grads, news, copies, means, squares = (results[5 * i : 5 * i + 5] for i in range(5))

    def store(n):
        copy = pltpu.make_async_copy(results[n], targets[n], out_sem.at[n])
        copy.start()
        stores.append(copy)

    def ready(*which):
        for n in which:
            loads[n].wait()

    def rows_through(n):
        pieces[n][0].wait()
        pieces[n][1].start()
        stores.append(pieces[n][1])

    ready(0, 1, 2, 5, 10, 15)
    roots = jnp.sqrt(tot[0:2, :])
    results[25][...] = roots[:, 0:10]
    store(25)
    ratio = learning_rate * (roots[0:1, :] / roots[1:2, :])

    def one(index, at, scale, grad, weight, first, second):
        update, mean_new, square_new = lamb_update(weight, grad, first, second)
        fresh = weight - scale * update
        for group, value in zip(
            (grads, news, copies, means, squares), (grad, fresh, fresh.astype(BF), mean_new, square_new)
        ):
            group[index][at] = value

    def send(index):
        for group in range(5):
            store(5 * group + index)

    one(2, Ellipsis, ratio[:, 4:5], gsh[1], w_up[...], m_up[...], v_up[...])
    send(2)
    ready(6, 11, 16)
    one(3, Ellipsis, ratio[:, 5:6], gsh[2], w_down[...], m_down[...], v_down[...])
    send(3)
    ready(3, 8, 13)
    attn = gsh[0]
    third = attn[:, 384:512]
    fourth = attn[:, 512:640]
    parts = (
        jnp.concatenate([attn[:, 0:128], third[:, 0:64]], axis=1),
        jnp.concatenate([attn[:, 128:256], fourth[:, 0:64]], axis=1),
        jnp.concatenate([attn[:, 256:384], third[:, 64:128]], axis=1),
    )
    for n in range(3):
        one(0, n, ratio[:, n : n + 1], parts[n], w_qkv[n], m_qkv[n], v_qkv[n])
    send(0)
    rows_through(0)
    rows_through(1)
    ready(4, 9, 14)
    out_grad = jnp.concatenate([attn[:, 640:768], fourth[:, 64:128]], axis=1).T
    one(1, Ellipsis, ratio[:, 3:4], out_grad, w_out[...], m_out[...], v_out[...])
    send(1)
    rows_through(2)
    rows_through(3)
    ready(7, 12, 17)
    for n in range(4):
        at = (slice(n, n + 1), slice(None))
        one(4, at, ratio[:, 6 + n : 7 + n], gn[n : n + 1, 0:96], w_norms[at], m_norms[at], v_norms[at])
    send(4)
    for copy in stores:
        copy.wait()


def fused_shards(
    captions, token_ids, pairing, low_images, high_images, frozen_qkv, frozen_out, frozen_up,
    frozen_down, frozen_gains, *state
):
    masters, firsts, seconds = state[0:5], state[5:10], state[10:15]
    cap_rows, seq_rows, width_all = captions.shape
    rows = cap_rows * seq_rows
    total_caps = cap_rows * lax.axis_size("dp")
    swapped = [
        tuple(a.T if n == 3 else a for n, a in enumerate(group)) for group in (masters, firsts, seconds)
    ]
    table = scratch_table()
    hbm = pl.BlockSpec(memory_space=pltpu.HBM)
    ins = dict(
        cap_h=captions.reshape(rows, width_all), tok_h=token_ids.T, pair_h=pairing.reshape(1, cap_rows),
        low_h=low_images.transpose(1, 0, 2), high_h=high_images, fqkv_h=frozen_qkv, fout_h=frozen_out,
        fup_h=frozen_up, fdown_h=frozen_down, fg_h=frozen_gains,
    )
    for key, group in zip(("m", "fi", "se"), swapped):
        ins.update(zip((key + part for part in ("q_h", "o_h", "u_h", "d_h", "n_h")), group))
    results = dict(
        ig_o=jax.ShapeDtypeStruct((rows, width_all), F32),
        gsh_o=jax.ShapeDtypeStruct((3, 96, width_all), F32),
        gn_o=jax.ShapeDtypeStruct((8, 128), F32),
        tot_o=jax.ShapeDtypeStruct((8, 128), F32),
    )
    names = tuple(ins) + tuple(results) + tuple(table)
    grad_in, gsh, gn, tot = pl.pallas_call(
        partial(step_kernel, names, total_caps),
        out_shape=tuple(results.values()),
        in_specs=[hbm] * len(ins),
        out_specs=tuple([hbm] * len(results)),
        scratch_shapes=list(table.values()),
        compiler_params=pltpu.CompilerParams(
            collective_id=0, has_side_effects=True, vmem_limit_bytes=62 * 1024 * 1024
        ),
    )(*ins.values())
    operands = (gsh, gn, tot, *swapped[0], *swapped[1], *swapped[2])
    shapes = [m.shape for m in swapped[0]]
    made = [jax.ShapeDtypeStruct(shape, kind) for kind in (F32, F32, BF, F32, F32) for shape in shapes]
    made.append(jax.ShapeDtypeStruct((2, 10), F32))
    outs = pl.pallas_call(
        lamb_kernel,
        out_shape=tuple(made) + (jax.ShapeDtypeStruct(grad_in.shape, F32),),
        in_specs=[hbm] * 19,
        out_specs=tuple([hbm] * 27),
        scratch_shapes=[pltpu.VMEM(a.shape, a.dtype) for a in operands]
        + [pltpu.VMEM(m.shape, m.dtype) for m in made]
        + [
            pltpu.VMEM(grad_in.shape, F32), pltpu.SemaphoreType.DMA((22,)), pltpu.SemaphoreType.DMA((30,))
        ],
        compiler_params=pltpu.CompilerParams(vmem_limit_bytes=62 * 1024 * 1024),
    )(*operands, grad_in)
    final = [out.T if n % 5 == 3 and n < 25 else out for n, out in enumerate(outs)]
    return (final[26].reshape(captions.shape), *final[:26])


def solution(mesh):
    whole = mesh.shape["dp"] == 8 and mesh.shape["mp"] == 4
    return jax.shard_map(
        fused_shards if whole else shards,
        mesh=mesh,
        in_specs=(
            P("dp", None, None),
            P("dp", None),
            P("dp"),
            P(("dp", "mp"), None, None),
            P(("dp", "mp"), None, None),
            P(),
            P(),
            P(),
            P(),
            P(),
            P(None, "dp", "mp"),
            P("mp", "dp"),
            P("dp", "mp"),
            P("mp", "dp"),
            P(None, "dp"),
            P(None, "dp", "mp"),
            P("mp", "dp"),
            P("dp", "mp"),
            P("mp", "dp"),
            P(None, "dp"),
            P(None, "dp", "mp"),
            P("mp", "dp"),
            P("dp", "mp"),
            P("mp", "dp"),
            P(None, "dp"),
        ),
        out_specs=(
            P("dp", None, None),
            P(None, "dp", "mp"),
            P("mp", "dp"),
            P("dp", "mp"),
            P("mp", "dp"),
            P(None, "dp"),
            P(None, "dp", "mp"),
            P("mp", "dp"),
            P("dp", "mp"),
            P("mp", "dp"),
            P(None, "dp"),
            P(None, "dp", "mp"),
            P("mp", "dp"),
            P("dp", "mp"),
            P("mp", "dp"),
            P(None, "dp"),
            P(None, "dp", "mp"),
            P("mp", "dp"),
            P("dp", "mp"),
            P("mp", "dp"),
            P(None, "dp"),
            P(None, "dp", "mp"),
            P("mp", "dp"),
            P("dp", "mp"),
            P("mp", "dp"),
            P(None, "dp"),
            P(),
        ),
        check_vma=False,
    )
```
